32 devices in a mesh: row: 4 (over y, x), col: 4 (over z), layer: 2 (over core).
Axes of the slice: x: 2, y: 2, z: 4, core: 2. Of those that a mesh axis runs over, the one named last changes fastest.
Arguments:
- density: bfloat16 [4096, 4096], P('row', ('col', 'layer')), as said below
- cotangent: bfloat16 [4096, 4096], P('row', ('col', 'layer')), may hold values from -6 to 6
- block_pattern: int32 [2, 362], replicated, may hold values from 0 to 31, as said below
Outputs:
- gradient: float32 [4096, 4096], P('row', ('col', 'layer'))
The draws below stay inside these ranges and needn't reach their ends.
Inputs may be any that keep to these rules, and one draw needn't show every extreme that they name: `block_pattern`: each column names one nonzero block; no block is named twice; every block (c, r) is listed with (r, c); all 32 diagonal blocks are listed, and 165 blocks above the diagonal. density is symmetric.
All inputs are finite; a program needn't handle non-finite values.
Results may differ from the reference program's by a relative error of at most 0.0025.
Values may be sent and summed in bfloat16 or wider, within the bound.
A program may use at most 128 MiB of HBM per device.

```python
import jax
import jax.numpy as jnp
import numpy as np

BS = 128
NB = 32
NN = 4096
OFF = 165


def draw_block_pattern(key, part):
    upper_a, upper_b = np.triu_indices(NB, 1)
    table_a = jnp.asarray(upper_a.astype(np.int32))
    table_b = jnp.asarray(upper_b.astype(np.int32))
    chosen = jax.random.permutation(jax.random.fold_in(key, 11), NB * (NB - 1) // 2)[:OFF]
    first = table_a[chosen]
    second = table_b[chosen]
    diagonal = jnp.arange(NB, dtype=jnp.int32)
    rows_list = jnp.concatenate([diagonal, first, second])
    cols_list = jnp.concatenate([diagonal, second, first])
    return jnp.stack([rows_list, cols_list]).astype(jnp.int32)


def draw_density(key, part):
    sigma = (NB * BS / 3.0) ** (-0.5)
    noise = jax.random.normal(jax.random.fold_in(key, 5), (NB * BS, NB * BS), jnp.float32)
    both = (noise + noise.T) * 0.5 ** 0.5 * sigma
    return both.astype(jnp.bfloat16)


def steps_of(stream_key, extent, pieces, least, top_value):
    def one(position, blocks):
        draws = jax.random.uniform(jax.random.fold_in(jax.random.fold_in(stream_key, 6), position), (blocks,), jnp.float32, least / len(pieces), top_value / len(pieces))
        return jnp.repeat(jnp.exp(draws), extent[position] // blocks).reshape((-1,) + (1,) * (len(extent) - position - 1))

    gain = one(*pieces[0])
    for cut in pieces[1:]:
        gain = gain * one(*cut)
    return gain


def centred(key, extent, spread, bound, split=(), held_as=jnp.bfloat16):
    drawn = spread * jax.random.normal(key, extent, jnp.float32)
    if split:
        drawn = drawn * steps_of(key, extent, split, -0.22, 0.18)
    return jnp.clip(drawn, -bound, bound).astype(held_as)


def setup_inputs(seed: int = 0) -> dict:
    keys = jax.random.split(jax.random.key(seed), 4)
    density = draw_density(jax.random.fold_in(keys[3], 71), 0)
    cotangent = centred(keys[1], (NN, NN), 1.0, 6.0, ((0, 4), (1, 8)))
    block_pattern = draw_block_pattern(jax.random.fold_in(keys[3], 71), 0)
    return {"density": density, "cotangent": cotangent, "block_pattern": block_pattern}


def reference(density, cotangent, block_pattern):
    blocks = jnp.zeros((NB, NB), jnp.float32).at[block_pattern[0], block_pattern[1]].set(1.0)
    mask = jnp.repeat(jnp.repeat(blocks, BS, axis=0), BS, axis=1) > 0.5
    xm = jnp.where(mask, density, jnp.zeros_like(density))
    square = jnp.where(mask, jnp.dot(xm, xm, preferred_element_type=jnp.float32), 0.0).astype(jnp.bfloat16)
    masked_grad = jnp.where(mask, cotangent, jnp.zeros_like(cotangent))
    grad_times = jnp.dot(masked_grad, xm, preferred_element_type=jnp.float32)
    pulled = jnp.where(mask, 3.0 * masked_grad.astype(jnp.float32) - 2.0 * grad_times, 0.0).astype(jnp.bfloat16)
    first_term = jnp.dot(square, masked_grad, preferred_element_type=jnp.float32)
    second_term = jnp.dot(pulled, xm, preferred_element_type=jnp.float32)
    third_term = jnp.dot(xm, pulled, preferred_element_type=jnp.float32)
    return jnp.where(mask, -2.0 * first_term + second_term + third_term, 0.0)
```

```python
import jax
import jax.numpy as jnp
from jax import lax
from jax.experimental import pallas as pl
from jax.experimental.pallas import tpu as pltpu
from jax.sharding import PartitionSpec as P

BS = 128
MESH = pl.DeviceIdType.MESH
ANY = pl.BlockSpec(memory_space=pl.ANY)


def ring_place(index, size):
    upper = index // (size // 2)
    return index + upper * (size + size // 2 - 1 - 2 * index)


class Spot:
    def __init__(self, rows, cols):
        self.rows, self.cols = rows, cols
        self.r = lax.axis_index("row")
        self.c = lax.axis_index("col")
        self.l = lax.axis_index("layer")
        self.p = ring_place(self.r, rows)
        self.right = (self.at(1), self.c, self.l)
        self.left = (self.at(-1), self.c, self.l)
        self.sibling = (self.r, self.c, 1 - self.l)
        self.up = (self.r, lax.rem(self.c + 1, cols), self.l)
        self.down = (self.r, lax.rem(self.c + cols - 1, cols), self.l)

    def at(self, step):
        return ring_place(lax.rem(self.p + step + self.rows, self.rows), self.rows)

    def greet(self, others):
        barrier = pltpu.get_barrier_semaphore()
        for other in others:
            pl.semaphore_signal(barrier, inc=1, device_id=other, device_id_type=MESH)
        pl.semaphore_wait(barrier, len(others))


def remote(src, dst, send, recv, device):
    return pltpu.make_async_remote_copy(
        src_ref=src, dst_ref=dst, send_sem=send, recv_sem=recv, device_id=device, device_id_type=MESH
    )


def ring_copies(spot, view, own, sends, recvs, item):
    half_way = spot.rows // 2
    tile = own.shape[0]
    steps = []
    for step in range(1, half_way + 1):
        pair = []
        for way, (target, sign) in enumerate(((spot.right, 1), (spot.left, -1))):
            origin = spot.at(-sign * (step - 1))
            if step < half_way:
                first, count = 0, tile
            else:
                first, count = way * (tile // 2), tile // 2
            src = own.at[pl.ds(first, count), :] if step == 1 else view(origin, first, count)
            pair.append(
                remote(
                    src,
                    view(origin, first, count),
                    sends.at[item, step - 1, way],
                    recvs.at[item, step - 1, way],
                    target,
                )
            )
        steps.append(pair)
    return steps


def gather_kernel(rows, cols, x_ref, g_ref, xr, xh, gr, gc, zs, zr, rs, rr, ss, sr, ls):
    spot = Spot(rows, cols)
    height, width = x_ref.shape
    c, l = spot.c, spot.l

    def wide(ref, col):
        return ref.at[:, pl.ds(pl.multiple_of((col * 2 + l) * width, width), width)]

    def x_view(col):
        def view(row, first, count):
            return xh.at[
                pl.ds(pl.multiple_of(row * height + first, 16), count),
                pl.ds(pl.multiple_of(col * width, width), width),
            ]

        return view

    def g_view(row, first, count):
        return gc.at[pl.ds(pl.multiple_of(row * height + first, 16), count), :]

    def x_mine(col):
        return x_view(col)(spot.r, 0, height)

    spot.greet((spot.right, spot.left, spot.sibling, spot.up, spot.down))

    items = [(0, 0)] + [(way, d) for d in range(1, cols) for way in (0, 1)]
    index_of = {item: i for i, item in enumerate(items)}

    def col_of(item):
        way, d = item
        return c - d if way == 0 else c + d

    def there(item):
        way, d = item
        if d == 0:
            return None
        return c >= d if way == 0 else c < cols - d

    def when(cond, body):
        if cond is None:
            body()
        else:
            pl.when(cond)(body)

    def both(a, b):
        return b if a is None else jnp.logical_and(a, b)

    def line_copy(kind, way, d):
        col = c - d if way == 0 else c + d
        own, view = (x_ref, x_mine) if kind == 0 else (g_ref, lambda k: wide(gr, k))
        src = own if d == 0 else view(col)
        target = spot.up if way == 0 else spot.down
        return remote(src, view(col), zs.at[kind, way, d], zr.at[kind, way, d], target)

    def line_sends(way, d):
        further = c < cols - 1 if way == 0 else c > 0
        return both(there((way, d)), further)

    def sibling_copy(kind, item):
        i = index_of[item]
        col = col_of(item)
        if kind == 0:
            src = x_ref if i == 0 else x_mine(col)
            dst = wide(xr, col)
        else:
            src = g_ref if i == 0 else wide(gr, col)
            dst = wide(gr, col)
        return remote(src, dst, ss.at[kind, i], sr.at[kind, i], spot.sibling)

    def sibling_arrival(kind, item):
        return sibling_copy(kind, item)

    def local_copy(item):
        i = index_of[item]
        col = col_of(item)
        src = x_ref if i == 0 else x_mine(col)
        return pltpu.make_async_copy(src, wide(xr, col), ls.at[i])

    def x_ring(item):
        return ring_copies(
            spot, x_view(col_of(item)), x_ref if item[1] == 0 else x_mine_ref(item), rs, rr, index_of[item]
        )

    def x_mine_ref(item):
        return x_mine(col_of(item))

    g_item = len(items)

    def g_ring():
        return ring_copies(spot, g_view, g_ref, rs, rr, g_item)

    def own_copies():
        return [
            pltpu.make_async_copy(x_ref, x_mine(c), ls.at[len(items)]),
            pltpu.make_async_copy(g_ref, wide(gr, c), ls.at[len(items) + 1]),
            pltpu.make_async_copy(g_ref, g_view(spot.r, 0, height), ls.at[len(items) + 2]),
        ]

    def start_pair(pair):
        for copy in pair:
            copy.start()

    def forward(steps, step):
        for way in (0, 1):
            steps[step - 1][way].wait_recv()
        start_pair(steps[step])

    ring_steps = rows // 2

    for way in (0, 1):
        when(line_sends(way, 0), lambda way=way: line_copy(0, way, 0).start())
    start_pair(x_ring((0, 0))[0])
    start_pair(g_ring()[0])
    for copy in own_copies():
        copy.start()
    for kind in (0, 1):
        sibling_copy(kind, (0, 0)).start()
    local_copy((0, 0)).start()
    for way in (0, 1):
        when(line_sends(way, 0), lambda way=way: line_copy(1, way, 0).start())

    def arrive_x(item):
        way, d = item
        line_copy(0, way, d - 1).wait_recv()
        when(line_sends(way, d) if d < cols - 1 else jnp.bool_(False), lambda: line_copy(0, way, d).start())
        start_pair(x_ring(item)[0])
        sibling_copy(0, item).start()
        local_copy(item).start()

    def arrive_g(item):
        way, d = item
        line_copy(1, way, d - 1).wait_recv()
        when(line_sends(way, d) if d < cols - 1 else jnp.bool_(False), lambda: line_copy(1, way, d).start())
        sibling_copy(1, item).start()

    def ring_on(item):
        steps = x_ring(item)
        for step in range(1, ring_steps):
            forward(steps, step)

    def g_ring_on():
        steps = g_ring()
        for step in range(1, ring_steps):
            forward(steps, step)

    for d in range(1, cols):
        for way in (0, 1):
            when(there((way, d)), lambda way=way, d=d: arrive_x((way, d)))
        if d == 1:
            ring_on((0, 0))
            g_ring_on()
        else:
            for way in (0, 1):
                when(there((way, d - 1)), lambda way=way, d=d: ring_on((way, d - 1)))
        for way in (0, 1):
            when(there((way, d)), lambda way=way, d=d: arrive_g((way, d)))
    for way in (0, 1):
        when(there((way, cols - 1)), lambda way=way: ring_on((way, cols - 1)))

    def finish(item):
        way, d = item
        steps = x_ring(item)
        for step in range(ring_steps):
            for copy in steps[step]:
                copy.wait_send()
        for copy in steps[-1]:
            copy.wait_recv()
        for kind in (0, 1):
            sibling_copy(kind, item).wait_send()
            sibling_copy(kind, item).wait_recv()
        local_copy(item).wait()

    for item in items:
        when(there(item), lambda item=item: finish(item))
    steps = g_ring()
    for step in range(ring_steps):
        for copy in steps[step]:
            copy.wait_send()
    for copy in steps[-1]:
        copy.wait_recv()
    for copy in own_copies():
        copy.wait()
    for kind in (0, 1):
        for way in (0, 1):
            for d in range(cols - 1):
                when(line_sends(way, d), lambda kind=kind, way=way, d=d: line_copy(kind, way, d).wait_send())


def share_kernel(rows, cols, width, s_ref, p_ref, sf, pf, pc, rs, rr, ss, sr, ls):
    spot = Spot(rows, cols)
    height = s_ref.shape[0]
    spot.greet((spot.right, spot.left, spot.sibling))
    mine = p_ref.at[:, pl.ds(pl.multiple_of(spot.c * width, width), width)]

    def view(row, first, count):
        return pc.at[pl.ds(pl.multiple_of(row * height + first, 16), count), :]

    steps = ring_copies(spot, view, mine, rs, rr, 0)
    for copy in steps[0]:
        copy.start()
    others = [pltpu.make_async_copy(mine, view(spot.r, 0, height), ls.at[2 * cols])]
    for kind, (half, full) in enumerate(((p_ref, pf), (s_ref, sf))):
        for col in range(cols):
            src = half.at[:, pl.ds(col * width, width)]
            dst = full.at[:, pl.ds(pl.multiple_of((col * 2 + spot.l) * width, width), width)]
            others.append(remote(src, dst, ss.at[kind, col], sr.at[kind, col], spot.sibling))
            others.append(pltpu.make_async_copy(src, dst, ls.at[kind * cols + col]))
    for copy in others:
        copy.start()
    for step in range(1, len(steps)):
        for copy in steps[step - 1]:
            copy.wait_recv()
        for copy in steps[step]:
            copy.start()
    for copy in steps[-1]:
        copy.wait_recv()
    for pair in steps:
        for copy in pair:
            copy.wait_send()
    for copy in others:
        copy.wait()


def gather_all(rows, cols, x, g):
    height, width = x.shape
    shape = lambda a, b: jax.ShapeDtypeStruct((a, b), x.dtype)
    items = 2 * cols - 1
    dma = pltpu.SemaphoreType.DMA
    return pl.pallas_call(
        lambda *refs: gather_kernel(rows, cols, *refs),
        out_shape=(
            shape(height, 2 * cols * width),
            shape(rows * height, cols * width),
            shape(height, 2 * cols * width),
            shape(rows * height, width),
        ),
        in_specs=[ANY] * 2,
        out_specs=(ANY,) * 4,
        scratch_shapes=[
            dma((2, 2, cols)),
            dma((2, 2, cols)),
            dma((items + 1, rows // 2, 2)),
            dma((items + 1, rows // 2, 2)),
            dma((2, items)),
            dma((2, items)),
            dma((items + 3,)),
        ],
        compiler_params=pltpu.CompilerParams(collective_id=0, has_side_effects=True),
        name="gather_all",
    )(x, g)


def share(rows, cols, width, s, p):
    height = s.shape[0]
    shape = lambda a, b: jax.ShapeDtypeStruct((a, b), s.dtype)
    dma = pltpu.SemaphoreType.DMA
    return pl.pallas_call(
        lambda *refs: share_kernel(rows, cols, width, *refs),
        out_shape=(
            shape(height, 2 * cols * width),
            shape(height, 2 * cols * width),
            shape(rows * height, width),
        ),
        in_specs=[ANY] * 2,
        out_specs=(ANY,) * 3,
        scratch_shapes=[
            dma((1, rows // 2, 2)),
            dma((1, rows // 2, 2)),
            dma((2, cols)),
            dma((2, cols)),
            dma((2 * cols + 1,)),
        ],
        compiler_params=pltpu.CompilerParams(collective_id=1, has_side_effects=True),
        name="share",
    )(s, p)


def dot(a, b):
    return jnp.dot(a, b, preferred_element_type=jnp.float32)


def hits(blocks, positions):
    return (blocks[:, None] == positions[None, :] // BS).astype(jnp.bfloat16)


def mask_of(block_pattern, row_positions, col_positions):
    counted = jnp.einsum(
        "nr,nc->rc",
        hits(block_pattern[0], row_positions),
        hits(block_pattern[1], col_positions),
        preferred_element_type=jnp.float32,
    )
    return counted > 0.5


def solution(mesh):
    rows, cols, layers = mesh.shape["row"], mesh.shape["col"], mesh.shape["layer"]

    def per_device(density, cotangent, block_pattern):
        height, width = density.shape
        r, c, l = (lax.axis_index(name) for name in ("row", "col", "layer"))
        row_at = r * height + jnp.arange(height, dtype=jnp.int32)
        col_at = (c * layers + l) * width + jnp.arange(width, dtype=jnp.int32)
        along = jnp.arange(cols * width, dtype=jnp.int32)
        half_at = ((along // width) * layers + l) * width + along % width
        mask = mask_of(block_pattern, row_at, col_at)
        half_mask = mask_of(block_pattern, row_at, half_at)
        xm = jnp.where(mask, density, jnp.zeros_like(density))
        masked_grad = jnp.where(mask, cotangent, jnp.zeros_like(cotangent))
        x_rows, x_half, g_rows, g_cols = gather_all(rows, cols, xm, masked_grad)
        g_half = lax.dynamic_index_in_dim(
            g_rows.reshape(height, cols, layers, width), l, axis=2, keepdims=False
        ).reshape(height, cols * width)
        square = jnp.where(half_mask, dot(x_rows, x_half), 0.0).astype(jnp.bfloat16)
        pulled = jnp.where(
            half_mask, 3.0 * g_half.astype(jnp.float32) - 2.0 * dot(g_rows, x_half), 0.0
        ).astype(jnp.bfloat16)
        s_rows, p_rows, p_cols = share(rows, cols, width, square, pulled)
        x_cols = lax.dynamic_slice_in_dim(x_half, c * width, width, axis=1)
        total = -2.0 * dot(s_rows, g_cols) + dot(p_rows, x_cols) + dot(x_rows, p_cols)
        return jnp.where(mask, total, 0.0)

    return jax.shard_map(
        per_device,
        mesh=mesh,
        in_specs=(P("row", ("col", "layer")), P("row", ("col", "layer")), P()),
        out_specs=P("row", ("col", "layer")),
        check_vma=False,
    )
```

```python
import jax
import jax.numpy as jnp
from jax import lax
from jax.experimental import pallas as pl
from jax.experimental.pallas import tpu as pltpu
from jax.sharding import PartitionSpec as P

BS = 128
MESH = pl.DeviceIdType.MESH
ANY = pl.BlockSpec(memory_space=pl.ANY)
VMEM = pl.BlockSpec(memory_space=pltpu.VMEM)
VMEM_LIMIT = 32 * 2**20


def ring_place(index, size):
    upper = index // (size // 2)
    return index + upper * (size + size // 2 - 1 - 2 * index)


class Spot:
    def __init__(self, rows, cols):
        self.rows, self.cols = rows, cols
        self.r = lax.axis_index("row")
        self.c = lax.axis_index("col")
        self.l = lax.axis_index("layer")
        self.p = ring_place(self.r, rows)
        self.right = (self.at(1), self.c, self.l)
        self.left = (self.at(-1), self.c, self.l)
        self.sibling = (self.r, self.c, 1 - self.l)
        self.up = (self.r, lax.rem(self.c + 1, cols), self.l)
        self.down = (self.r, lax.rem(self.c + cols - 1, cols), self.l)

    def at(self, step):
        return ring_place(lax.rem(self.p + step + self.rows, self.rows), self.rows)

    def greet(self, others):
        barrier = pltpu.get_barrier_semaphore()
        for other in others:
            pl.semaphore_signal(barrier, inc=1, device_id=other, device_id_type=MESH)
        pl.semaphore_wait(barrier, len(others))


def remote(src, dst, send, recv, device):
    return pltpu.make_async_remote_copy(
        src_ref=src, dst_ref=dst, send_sem=send, recv_sem=recv, device_id=device, device_id_type=MESH
    )


def ring_copies(spot, view, own, sends, recvs, item):
    half_way = spot.rows // 2
    tile = own.shape[0]
    steps = []
    for step in range(1, half_way + 1):
        pair = []
        for way, (target, sign) in enumerate(((spot.right, 1), (spot.left, -1))):
            origin = spot.at(-sign * (step - 1))
            if step < half_way:
                first, count = 0, tile
            else:
                first, count = way * (tile // 2), tile // 2
            src = own.at[pl.ds(first, count), :] if step == 1 else view(origin, first, count)
            pair.append(
                remote(
                    src,
                    view(origin, first, count),
                    sends.at[item, step - 1, way],
                    recvs.at[item, step - 1, way],
                    target,
                )
            )
        steps.append(pair)
    return steps


def gather_kernel(rows, cols, x_ref, g_ref, xr, xh, gr, gh, gc, xs, gs, zs, zr, rs, rr, ss, sr, ls):
    spot = Spot(rows, cols)
    height, width = x_ref.shape
    c, l = spot.c, spot.l

    def wide(ref, col):
        return ref.at[:, pl.ds(pl.multiple_of((col * 2 + l) * width, width), width)]

    def x_view(col):
        def view(row, first, count):
            return xh.at[
                pl.ds(pl.multiple_of(row * height + first, 16), count),
                pl.ds(pl.multiple_of(col * width, width), width),
            ]

        return view

    def g_view(row, first, count):
        return gc.at[pl.ds(pl.multiple_of(row * height + first, 16), count), :]

    def slot(kind, col):
        return (xs, gs)[kind].at[col]

    def tile_of(kind, item):
        if item[1] == 0:
            return (x_ref, g_ref)[kind]
        return slot(kind, col_of(item))

    spot.greet((spot.right, spot.left, spot.sibling, spot.up, spot.down))

    items = [(0, 0)] + [(way, d) for d in range(1, cols) for way in (0, 1)]
    index_of = {item: i for i, item in enumerate(items)}

    def col_of(item):
        way, d = item
        return c - d if way == 0 else c + d

    def there(item):
        way, d = item
        if d == 0:
            return None
        return c >= d if way == 0 else c < cols - d

    def when(cond, body):
        if cond is None:
            body()
        else:
            pl.when(cond)(body)

    def both(a, b):
        return b if a is None else jnp.logical_and(a, b)

    def line_copy(kind, way, d):
        col = c - d if way == 0 else c + d
        src = tile_of(kind, (way, d))
        target = spot.up if way == 0 else spot.down
        return remote(src, slot(kind, col), zs.at[kind, way, d], zr.at[kind, way, d], target)

    def line_sends(way, d):
        further = c < cols - 1 if way == 0 else c > 0
        return both(there((way, d)), further)

    def sibling_copy(kind, item):
        i = index_of[item]
        dst = wide((xr, gr)[kind], col_of(item))
        return remote(tile_of(kind, item), dst, ss.at[kind, i], sr.at[kind, i], spot.sibling)

    def local_copies(kind, item):
        i = index_of[item]
        col = col_of(item)
        src = tile_of(kind, item)
        if kind == 0:
            targets = (wide(xr, col), x_view(col)(spot.r, 0, height))
        else:
            targets = (wide(gr, col), gh.at[:, pl.ds(pl.multiple_of(col * width, width), width)])
        return [pltpu.make_async_copy(src, dst, ls.at[kind, j, i]) for j, dst in enumerate(targets)]

    def x_ring(item):
        return ring_copies(spot, x_view(col_of(item)), tile_of(0, item), rs, rr, index_of[item])

    g_item = len(items)

    def g_ring():
        return ring_copies(spot, g_view, g_ref, rs, rr, g_item)

    def g_col_copy():
        return pltpu.make_async_copy(g_ref, g_view(spot.r, 0, height), ls.at[0, 0, len(items)])

    def start_pair(pair):
        for copy in pair:
            copy.start()

    def forward(steps, step):
        for way in (0, 1):
            steps[step - 1][way].wait_recv()
        start_pair(steps[step])

    ring_steps = rows // 2

    def spread(kind, item):
        sibling_copy(kind, item).start()
        for copy in local_copies(kind, item):
            copy.start()

    for way in (0, 1):
        when(line_sends(way, 0), lambda way=way: line_copy(0, way, 0).start())
    start_pair(x_ring((0, 0))[0])
    start_pair(g_ring()[0])
    g_col_copy().start()
    for kind in (0, 1):
        spread(kind, (0, 0))
    for way in (0, 1):
        when(line_sends(way, 0), lambda way=way: line_copy(1, way, 0).start())

    def arrive_x(item):
        way, d = item
        line_copy(0, way, d - 1).wait_recv()
        when(line_sends(way, d) if d < cols - 1 else jnp.bool_(False), lambda: line_copy(0, way, d).start())
        start_pair(x_ring(item)[0])
        spread(0, item)

    def arrive_g(item):
        way, d = item
        line_copy(1, way, d - 1).wait_recv()
        when(line_sends(way, d) if d < cols - 1 else jnp.bool_(False), lambda: line_copy(1, way, d).start())
        spread(1, item)

    def ring_on(item):
        steps = x_ring(item)
        for step in range(1, ring_steps):
            forward(steps, step)

    def g_ring_on():
        steps = g_ring()
        for step in range(1, ring_steps):
            forward(steps, step)

    for d in range(1, cols):
        for way in (0, 1):
            when(there((way, d)), lambda way=way, d=d: arrive_x((way, d)))
        if d == 1:
            ring_on((0, 0))
            g_ring_on()
        else:
            for way in (0, 1):
                when(there((way, d - 1)), lambda way=way, d=d: ring_on((way, d - 1)))
        for way in (0, 1):
            when(there((way, d)), lambda way=way, d=d: arrive_g((way, d)))
    for way in (0, 1):
        when(there((way, cols - 1)), lambda way=way: ring_on((way, cols - 1)))

    def finish(item):
        way, d = item
        steps = x_ring(item)
        for step in range(ring_steps):
            for copy in steps[step]:
                copy.wait_send()
        for copy in steps[-1]:
            copy.wait_recv()
        for kind in (0, 1):
            copy = sibling_copy(kind, item)
            copy.wait_send()
            copy.wait_recv()
            for copy in local_copies(kind, item):
                copy.wait()

    for item in items:
        when(there(item), lambda item=item: finish(item))
    steps = g_ring()
    for step in range(ring_steps):
        for copy in steps[step]:
            copy.wait_send()
    for copy in steps[-1]:
        copy.wait_recv()
    g_col_copy().wait()
    for kind in (0, 1):
        for way in (0, 1):
            for d in range(cols - 1):
                when(line_sends(way, d), lambda kind=kind, way=way, d=d: line_copy(kind, way, d).wait_send())


def share_kernel(rows, cols, width, s_ref, p_ref, sf, pf, pc, rs, rr, ss, sr, ls):
    spot = Spot(rows, cols)
    height = s_ref.shape[0]
    spot.greet((spot.right, spot.left, spot.sibling))
    mine = p_ref.at[:, pl.ds(pl.multiple_of(spot.c * width, width), width)]

    def view(row, first, count):
        return pc.at[pl.ds(pl.multiple_of(row * height + first, 16), count), :]

    steps = ring_copies(spot, view, mine, rs, rr, 0)
    for copy in steps[0]:
        copy.start()
    others = [pltpu.make_async_copy(mine, view(spot.r, 0, height), ls.at[2 * cols])]
    for kind, (half, full) in enumerate(((p_ref, pf), (s_ref, sf))):
        for col in range(cols):
            src = half.at[:, pl.ds(col * width, width)]
            dst = full.at[:, pl.ds(pl.multiple_of((col * 2 + spot.l) * width, width), width)]
            others.append(remote(src, dst, ss.at[kind, col], sr.at[kind, col], spot.sibling))
            others.append(pltpu.make_async_copy(src, dst, ls.at[kind * cols + col]))
    for copy in others:
        copy.start()
    for step in range(1, len(steps)):
        for copy in steps[step - 1]:
            copy.wait_recv()
        for copy in steps[step]:
            copy.start()
    for copy in steps[-1]:
        copy.wait_recv()
    for pair in steps:
        for copy in pair:
            copy.wait_send()
    for copy in others:
        copy.wait()


def gather_all(rows, cols, x, g):
    height, width = x.shape
    shape = lambda a, b: jax.ShapeDtypeStruct((a, b), x.dtype)
    items = 2 * cols - 1
    dma = pltpu.SemaphoreType.DMA
    return pl.pallas_call(
        lambda *refs: gather_kernel(rows, cols, *refs),
        out_shape=(
            shape(height, 2 * cols * width),
            shape(rows * height, cols * width),
            shape(height, 2 * cols * width),
            shape(height, cols * width),
            shape(rows * height, width),
        ),
        in_specs=[VMEM] * 2,
        out_specs=(ANY,) * 5,
        scratch_shapes=[
            pltpu.VMEM((cols, height, width), x.dtype),
            pltpu.VMEM((cols, height, width), x.dtype),
            dma((2, 2, cols)),
            dma((2, 2, cols)),
            dma((items + 1, rows // 2, 2)),
            dma((items + 1, rows // 2, 2)),
            dma((2, items)),
            dma((2, items)),
            dma((2, 2, items + 1)),
        ],
        compiler_params=pltpu.CompilerParams(collective_id=0, has_side_effects=True, vmem_limit_bytes=VMEM_LIMIT),
        name="gather_all",
    )(x, g)


def share(rows, cols, width, s, p):
    height = s.shape[0]
    shape = lambda a, b: jax.ShapeDtypeStruct((a, b), s.dtype)
    dma = pltpu.SemaphoreType.DMA
    return pl.pallas_call(
        lambda *refs: share_kernel(rows, cols, width, *refs),
        out_shape=(
            shape(height, 2 * cols * width),
            shape(height, 2 * cols * width),
            shape(rows * height, width),
        ),
        in_specs=[VMEM] * 2,
        out_specs=(ANY,) * 3,
        scratch_shapes=[
            dma((1, rows // 2, 2)),
            dma((1, rows // 2, 2)),
            dma((2, cols)),
            dma((2, cols)),
            dma((2 * cols + 1,)),
        ],
        compiler_params=pltpu.CompilerParams(collective_id=1, has_side_effects=True, vmem_limit_bytes=VMEM_LIMIT),
        name="share",
    )(s, p)


def dot(a, b):
    return jnp.dot(a, b, preferred_element_type=jnp.float32)


def hits(blocks, positions):
    return (blocks[:, None] == positions[None, :] // BS).astype(jnp.bfloat16)


def mask_of(block_pattern, row_positions, col_positions):
    counted = jnp.einsum(
        "nr,nc->rc",
        hits(block_pattern[0], row_positions),
        hits(block_pattern[1], col_positions),
        preferred_element_type=jnp.float32,
    )
    return counted > 0.5


def solution(mesh):
    rows, cols, layers = mesh.shape["row"], mesh.shape["col"], mesh.shape["layer"]

    def per_device(density, cotangent, block_pattern):
        height, width = density.shape
        r, c, l = (lax.axis_index(name) for name in ("row", "col", "layer"))
        row_at = r * height + jnp.arange(height, dtype=jnp.int32)
        col_at = (c * layers + l) * width + jnp.arange(width, dtype=jnp.int32)
        along = jnp.arange(cols * width, dtype=jnp.int32)
        half_at = ((along // width) * layers + l) * width + along % width
        mask = mask_of(block_pattern, row_at, col_at)
        half_mask = mask_of(block_pattern, row_at, half_at)
        xm = jnp.where(mask, density, jnp.zeros_like(density))
        masked_grad = jnp.where(mask, cotangent, jnp.zeros_like(cotangent))
        x_rows, x_half, g_rows, g_half, g_cols = gather_all(rows, cols, xm, masked_grad)
        square = jnp.where(half_mask, dot(x_rows, x_half), 0.0).astype(jnp.bfloat16)
        pulled = jnp.where(
            half_mask, 3.0 * g_half.astype(jnp.float32) - 2.0 * dot(g_rows, x_half), 0.0
        ).astype(jnp.bfloat16)
        s_rows, p_rows, p_cols = share(rows, cols, width, square, pulled)
        x_cols = lax.dynamic_slice_in_dim(x_half, c * width, width, axis=1)
        total = -2.0 * dot(s_rows, g_cols) + dot(p_rows, x_cols) + dot(x_rows, p_cols)
        return jnp.where(mask, total, 0.0)

    return jax.shard_map(
        per_device,
        mesh=mesh,
        in_specs=(P("row", ("col", "layer")), P("row", ("col", "layer")), P()),
        out_specs=P("row", ("col", "layer")),
        check_vma=False,
    )
```

```python
import jax
import jax.numpy as jnp
from jax import lax
from jax.experimental import pallas as pl
from jax.experimental.pallas import tpu as pltpu
from jax.sharding import PartitionSpec as P

BS = 128
MESH = pl.DeviceIdType.MESH
ANY = pl.BlockSpec(memory_space=pl.ANY)
VMEM = pl.BlockSpec(memory_space=pltpu.VMEM)
VMEM_LIMIT = 48 * 2**20


def ring_place(index, size):
    upper = index // (size // 2)
    return index + upper * (size + size // 2 - 1 - 2 * index)


class Spot:
    def __init__(self, rows, cols):
        self.rows, self.cols = rows, cols
        self.r = lax.axis_index("row")
        self.c = lax.axis_index("col")
        self.l = lax.axis_index("layer")
        self.p = ring_place(self.r, rows)
        self.right = (self.at(1), self.c, self.l)
        self.left = (self.at(-1), self.c, self.l)
        self.sibling = (self.r, self.c, 1 - self.l)
        self.up = (self.r, lax.rem(self.c + 1, cols), self.l)
        self.down = (self.r, lax.rem(self.c + cols - 1, cols), self.l)

    def at(self, step):
        return ring_place(lax.rem(self.p + step + self.rows, self.rows), self.rows)

    def greet(self, others):
        barrier = pltpu.get_barrier_semaphore()
        for other in others:
            pl.semaphore_signal(barrier, inc=1, device_id=other, device_id_type=MESH)
        pl.semaphore_wait(barrier, len(others))


def remote(src, dst, send, recv, device):
    return pltpu.make_async_remote_copy(
        src_ref=src, dst_ref=dst, send_sem=send, recv_sem=recv, device_id=device, device_id_type=MESH
    )


def ring_copies(spot, view, own, sends, recvs, item, only=None):
    half_way = spot.rows // 2
    tile = own.shape[0]
    steps = []
    for step in range(1, half_way + 1):
        pair = []
        for way, (target, sign) in enumerate(((spot.right, 1), (spot.left, -1))):
            origin = spot.at(-sign * (step - 1))
            if step < half_way:
                first, count = 0, tile
            else:
                first, count = way * (tile // 2), tile // 2
            src = own.at[pl.ds(first, count), :] if step == 1 else view(origin, first, count)
            copy = remote(
                src,
                view(origin, first, count),
                sends.at[item, step - 1, way],
                recvs.at[item, step - 1, way],
                target,
            )
            if only is None:
                pair.append((copy, None, None))
            else:
                pair.append((copy, origin == only, spot.at(-sign * step) == only))
        steps.append(pair)
    return steps


def when(cond, body):
    if cond is None:
        body()
    else:
        pl.when(cond)(body)


def start_pair(pair):
    for copy, sent, _ in pair:
        when(sent, copy.start)


def pair_arrives(pair):
    for copy, _, arrives in pair:
        when(arrives, copy.wait_recv)


def pair_left(pair):
    for copy, sent, _ in pair:
        when(sent, copy.wait_send)


def pass_on(steps):
    for step in range(1, len(steps)):
        pair_arrives(steps[step - 1])
        start_pair(steps[step])


def gather_kernel(
    rows, cols, x_ref, g_ref, xr, xh, gr, gh, gc, xs, gs, zs, zr, rs, rr, ss, sr, ls, *symmetric
):
    spot = Spot(rows, cols)
    height, width = x_ref.shape
    c, l = spot.c, spot.l

    def wide(ref, col):
        return ref.at[:, pl.ds(pl.multiple_of((col * 2 + l) * width, width), width)]

    def x_view(col):
        def view(row, first, count):
            return xh.at[
                pl.ds(pl.multiple_of(row * height + first, 16), count),
                pl.ds(pl.multiple_of(col * width, width), width),
            ]

        return view

    def g_view(row, first, count):
        return gc.at[pl.ds(pl.multiple_of(row * height + first, 16), count), :]

    def slot(kind, col):
        return (xs, gs)[kind].at[col]

    def tile_of(kind, item):
        if item[1] == 0:
            return (x_ref, g_ref)[kind]
        return slot(kind, col_of(item))

    spot.greet((spot.right, spot.left, spot.sibling, spot.up, spot.down))

    items = [(0, 0)] + [(way, d) for d in range(1, cols) for way in (0, 1)]
    index_of = {item: i for i, item in enumerate(items)}

    def col_of(item):
        way, d = item
        return c - d if way == 0 else c + d

    def there(item):
        way, d = item
        if d == 0:
            return None
        return c >= d if way == 0 else c < cols - d

    def both(a, b):
        return b if a is None else jnp.logical_and(a, b)

    def line_copy(kind, way, d):
        col = c - d if way == 0 else c + d
        src = tile_of(kind, (way, d))
        target = spot.up if way == 0 else spot.down
        return remote(src, slot(kind, col), zs.at[kind, way, d], zr.at[kind, way, d], target)

    def line_sends(way, d):
        further = c < cols - 1 if way == 0 else c > 0
        return both(there((way, d)), further)

    def sibling_copy(kind, item):
        i = index_of[item]
        dst = wide((xr, gr)[kind], col_of(item))
        return remote(tile_of(kind, item), dst, ss.at[kind, i], sr.at[kind, i], spot.sibling)

    def local_copies(kind, item):
        i = index_of[item]
        col = col_of(item)
        src = tile_of(kind, item)
        if kind == 0:
            targets = (wide(xr, col), x_view(col)(spot.r, 0, height))
        else:
            targets = (wide(gr, col), gh.at[:, pl.ds(pl.multiple_of(col * width, width), width)])
        return [pltpu.make_async_copy(src, dst, ls.at[kind, j, i]) for j, dst in enumerate(targets)]

    if symmetric:
        rb, eb, tb, es, er, ts, tr, dl = symmetric

    def sent_half(row, col):
        return l + (row < col).astype(jnp.int32) * (1 - 2 * l)

    def rows_at(tile, half):
        return tile.at[pl.ds(pl.multiple_of(half * width, width), width), :]

    def x_rings(item):
        i, col, tile = index_of[item], col_of(item), tile_of(0, item)
        if not symmetric:
            return [ring_copies(spot, x_view(col), tile, rs, rr, i)]

        def view(row, first, count):
            return rb.at[row, col, pl.ds(first, count), :]

        def extra_view(row, first, count):
            return eb.at[col, pl.ds(first, count), :]

        half = sent_half(spot.r, col)
        return [
            ring_copies(spot, view, rows_at(tile, half), rs, rr, i),
            ring_copies(spot, extra_view, rows_at(tile, 1 - half), es, er, i, only=col),
        ]

    def x_start(item):
        for steps in x_rings(item):
            start_pair(steps[0])

    def turned(item, offset, row):
        i, col = index_of[item], col_of(item)
        src = tb.at[row, col]
        dst = xh.at[
            pl.ds(pl.multiple_of(col * height + l * width, width), width),
            pl.ds(pl.multiple_of(row * width, width), width),
        ]
        return (
            pltpu.make_async_copy(src, dst, dl.at[1, offset, i]),
            remote(src, dst, ts.at[offset, i], tr.at[offset, i], spot.sibling),
        )

    def placed(item, offset, row):
        i, col = index_of[item], col_of(item)
        half = sent_half(row, col)

        def target(h):
            return x_view(col)(row, h * width, width)

        return (
            pltpu.make_async_copy(rb.at[row, col], target(half), dl.at[0, offset, i]),
            pltpu.make_async_copy(eb.at[col], target(1 - half), dl.at[2, 0, i]),
        )

    def turn(item, offset, row, src):
        col = col_of(item)

        @pl.when(jnp.logical_and(row != col, col != spot.r))
        def _():
            @pl.loop(0, width // BS)
            def _(strip):
                at = pl.ds(pl.multiple_of(strip * BS, BS), BS)
                tb[row, col, at, :] = src[:, at].T

            here, there_ = turned(item, offset, row)
            pl.when(row > col)(here.start)
            pl.when(row < col)(there_.start)

    def turn_done(item, offset, row):
        col = col_of(item)

        @pl.when(jnp.logical_and(row != col, col != spot.r))
        def _():
            here, there_ = turned(item, offset, row)
            pl.when(row > col)(here.wait)
            pl.when(row < col)(there_.wait)

    def turn_own(item):
        if symmetric:
            half = sent_half(spot.r, col_of(item))
            turn(item, 0, spot.r, rows_at(tile_of(0, item), half))

    def take(item):
        for steps in x_rings(item):
            pair_arrives(steps[-1])
        if symmetric:

            @pl.loop(1, rows)
            def _(offset):
                row = spot.at(offset)
                tile, extra = placed(item, offset, row)
                tile.start()
                pl.when(row == col_of(item))(extra.start)
                turn(item, offset, row, rb.at[row, col_of(item)])

    def take_done(item):
        if symmetric:
            turn_done(item, 0, spot.r)

            @pl.loop(1, rows)
            def _(offset):
                row = spot.at(offset)
                tile, extra = placed(item, offset, row)
                tile.wait()
                pl.when(row == col_of(item))(extra.wait)
                turn_done(item, offset, row)

    g_item = len(items)

    def g_ring():
        return ring_copies(spot, g_view, g_ref, rs, rr, g_item)

    def g_col_copy():
        return pltpu.make_async_copy(g_ref, g_view(spot.r, 0, height), ls.at[0, 0, len(items)])

    def spread(kind, item):
        sibling_copy(kind, item).start()
        for copy in local_copies(kind, item):
            copy.start()

    for way in (0, 1):
        when(line_sends(way, 0), lambda way=way: line_copy(0, way, 0).start())
    x_start((0, 0))
    start_pair(g_ring()[0])
    g_col_copy().start()
    for kind in (0, 1):
        spread(kind, (0, 0))
    for way in (0, 1):
        when(line_sends(way, 0), lambda way=way: line_copy(1, way, 0).start())

    def arrive_x(item):
        way, d = item
        line_copy(0, way, d - 1).wait_recv()
        when(line_sends(way, d) if d < cols - 1 else jnp.bool_(False), lambda: line_copy(0, way, d).start())
        x_start(item)
        spread(0, item)

    def arrive_g(item):
        way, d = item
        line_copy(1, way, d - 1).wait_recv()
        when(line_sends(way, d) if d < cols - 1 else jnp.bool_(False), lambda: line_copy(1, way, d).start())
        spread(1, item)

    def ring_on(item):
        for steps in x_rings(item):
            pass_on(steps)

    turn_own((0, 0))
    previous = [(0, 0)]
    def each(some, body):
        for item in some:
            when(there(item), lambda item=item: body(item))

    for d in range(1, cols):
        current = [(0, d), (1, d)]
        each(current, arrive_x)
        each(previous, ring_on)
        if d == 1:
            pass_on(g_ring())
        each(current, turn_own)
        each(current, arrive_g)
        each(previous, take)
        previous = current
    each(previous, ring_on)
    each(previous, take)

    def finish(item):
        way, d = item
        for steps in x_rings(item):
            for pair in steps:
                pair_left(pair)
        take_done(item)
        for kind in (0, 1):
            copy = sibling_copy(kind, item)
            copy.wait_send()
            copy.wait_recv()
            for copy in local_copies(kind, item):
                copy.wait()

    each(items, finish)
    steps = g_ring()
    for pair in steps:
        pair_left(pair)
    pair_arrives(steps[-1])
    g_col_copy().wait()
    for kind in (0, 1):
        for way in (0, 1):
            for d in range(cols - 1):
                when(line_sends(way, d), lambda kind=kind, way=way, d=d: line_copy(kind, way, d).wait_send())


def share_kernel(rows, cols, width, s_ref, p_ref, sf, pf, pc, rs, rr, ss, sr, ls):
    spot = Spot(rows, cols)
    height = s_ref.shape[0]
    spot.greet((spot.right, spot.left, spot.sibling))
    mine = p_ref.at[:, pl.ds(pl.multiple_of(spot.c * width, width), width)]

    def view(row, first, count):
        return pc.at[pl.ds(pl.multiple_of(row * height + first, 16), count), :]

    steps = ring_copies(spot, view, mine, rs, rr, 0)
    start_pair(steps[0])
    others = [pltpu.make_async_copy(mine, view(spot.r, 0, height), ls.at[2 * cols])]
    for kind, (half, full) in enumerate(((p_ref, pf), (s_ref, sf))):
        for col in range(cols):
            src = half.at[:, pl.ds(col * width, width)]
            dst = full.at[:, pl.ds(pl.multiple_of((col * 2 + spot.l) * width, width), width)]
            others.append(remote(src, dst, ss.at[kind, col], sr.at[kind, col], spot.sibling))
            others.append(pltpu.make_async_copy(src, dst, ls.at[kind * cols + col]))
    for copy in others:
        copy.start()
    pass_on(steps)
    pair_arrives(steps[-1])
    for pair in steps:
        pair_left(pair)
    for copy in others:
        copy.wait()


def gather_all(rows, cols, x, g):
    height, width = x.shape
    shape = lambda a, b: jax.ShapeDtypeStruct((a, b), x.dtype)
    items = 2 * cols - 1
    dma = pltpu.SemaphoreType.DMA
    symmetric = []
    if height == 2 * width and rows == cols:
        symmetric = [
            pltpu.VMEM((rows, cols, width, width), x.dtype),
            pltpu.VMEM((cols, width, width), x.dtype),
            pltpu.VMEM((rows, cols, width, width), x.dtype),
            dma((items, rows // 2, 2)),
            dma((items, rows // 2, 2)),
            dma((rows, items)),
            dma((rows, items)),
            dma((3, rows, items)),
        ]
    return pl.pallas_call(
        lambda *refs: gather_kernel(rows, cols, *refs),
        out_shape=(
            shape(height, 2 * cols * width),
            shape(rows * height, cols * width),
            shape(height, 2 * cols * width),
            shape(height, cols * width),
            shape(rows * height, width),
        ),
        in_specs=[VMEM] * 2,
        out_specs=(ANY,) * 5,
        scratch_shapes=[
            pltpu.VMEM((cols, height, width), x.dtype),
            pltpu.VMEM((cols, height, width), x.dtype),
            dma((2, 2, cols)),
            dma((2, 2, cols)),
            dma((items + 1, rows // 2, 2)),
            dma((items + 1, rows // 2, 2)),
            dma((2, items)),
            dma((2, items)),
            dma((2, 2, items + 1)),
            *symmetric,
        ],
        compiler_params=pltpu.CompilerParams(collective_id=0, has_side_effects=True, vmem_limit_bytes=VMEM_LIMIT),
        name="gather_all",
    )(x, g)


def share(rows, cols, width, s, p):
    height = s.shape[0]
    shape = lambda a, b: jax.ShapeDtypeStruct((a, b), s.dtype)
    dma = pltpu.SemaphoreType.DMA
    return pl.pallas_call(
        lambda *refs: share_kernel(rows, cols, width, *refs),
        out_shape=(
            shape(height, 2 * cols * width),
            shape(height, 2 * cols * width),
            shape(rows * height, width),
        ),
        in_specs=[VMEM] * 2,
        out_specs=(ANY,) * 3,
        scratch_shapes=[
            dma((1, rows // 2, 2)),
            dma((1, rows // 2, 2)),
            dma((2, cols)),
            dma((2, cols)),
            dma((2 * cols + 1,)),
        ],
        compiler_params=pltpu.CompilerParams(collective_id=1, has_side_effects=True, vmem_limit_bytes=VMEM_LIMIT),
        name="share",
    )(s, p)


def dot(a, b):
    return jnp.dot(a, b, preferred_element_type=jnp.float32)


def hits(blocks, positions):
    return (blocks[:, None] == positions[None, :] // BS).astype(jnp.bfloat16)


def mask_of(block_pattern, row_positions, col_positions):
    counted = jnp.einsum(
        "nr,nc->rc",
        hits(block_pattern[0], row_positions),
        hits(block_pattern[1], col_positions),
        preferred_element_type=jnp.float32,
    )
    return counted > 0.5


def solution(mesh):
    rows, cols, layers = mesh.shape["row"], mesh.shape["col"], mesh.shape["layer"]

    def per_device(density, cotangent, block_pattern):
        height, width = density.shape
        r, c, l = (lax.axis_index(name) for name in ("row", "col", "layer"))
        row_at = r * height + jnp.arange(height, dtype=jnp.int32)
        col_at = (c * layers + l) * width + jnp.arange(width, dtype=jnp.int32)
        along = jnp.arange(cols * width, dtype=jnp.int32)
        half_at = ((along // width) * layers + l) * width + along % width
        mask = mask_of(block_pattern, row_at, col_at)
        half_mask = mask_of(block_pattern, row_at, half_at)
        xm = jnp.where(mask, density, jnp.zeros_like(density))
        masked_grad = jnp.where(mask, cotangent, jnp.zeros_like(cotangent))
        x_rows, x_half, g_rows, g_half, g_cols = gather_all(rows, cols, xm, masked_grad)
        square = jnp.where(half_mask, dot(x_rows, x_half), 0.0).astype(jnp.bfloat16)
        pulled = jnp.where(
            half_mask, 3.0 * g_half.astype(jnp.float32) - 2.0 * dot(g_rows, x_half), 0.0
        ).astype(jnp.bfloat16)
        s_rows, p_rows, p_cols = share(rows, cols, width, square, pulled)
        x_cols = lax.dynamic_slice_in_dim(x_half, c * width, width, axis=1)
        total = -2.0 * dot(s_rows, g_cols) + dot(p_rows, x_cols) + dot(x_rows, p_cols)
        return jnp.where(mask, total, 0.0)

    return jax.shard_map(
        per_device,
        mesh=mesh,
        in_specs=(P("row", ("col", "layer")), P("row", ("col", "layer")), P()),
        out_specs=P("row", ("col", "layer")),
        check_vma=False,
    )
```

```python
import jax
import jax.numpy as jnp
from jax import lax
from jax.experimental import pallas as pl
from jax.experimental.pallas import tpu as pltpu
from jax.sharding import PartitionSpec as P

BS = 128
MESH = pl.DeviceIdType.MESH
ANY = pl.BlockSpec(memory_space=pl.ANY)
VMEM = pl.BlockSpec(memory_space=pltpu.VMEM)
VMEM_LIMIT = 48 * 2**20


def ring_place(index, size):
    upper = index // (size // 2)
    return index + upper * (size + size // 2 - 1 - 2 * index)


class Spot:
    def __init__(self, rows, cols):
        self.rows, self.cols = rows, cols
        self.r = lax.axis_index("row")
        self.c = lax.axis_index("col")
        self.l = lax.axis_index("layer")
        self.p = ring_place(self.r, rows)
        self.right = (self.at(1), self.c, self.l)
        self.left = (self.at(-1), self.c, self.l)
        self.sibling = (self.r, self.c, 1 - self.l)
        self.up = (self.r, lax.rem(self.c + 1, cols), self.l)
        self.down = (self.r, lax.rem(self.c + cols - 1, cols), self.l)

    def at(self, step):
        return ring_place(lax.rem(self.p + step + self.rows, self.rows), self.rows)

    def greet(self, others):
        barrier = pltpu.get_barrier_semaphore()
        for other in others:
            pl.semaphore_signal(barrier, inc=1, device_id=other, device_id_type=MESH)
        pl.semaphore_wait(barrier, len(others))


def remote(src, dst, send, recv, device):
    return pltpu.make_async_remote_copy(
        src_ref=src, dst_ref=dst, send_sem=send, recv_sem=recv, device_id=device, device_id_type=MESH
    )


def ring_copies(spot, view, own, sends, recvs, item, only=None):
    half_way = spot.rows // 2
    tile = own.shape[0]
    steps = []
    for step in range(1, half_way + 1):
        pair = []
        for way, (target, sign) in enumerate(((spot.right, 1), (spot.left, -1))):
            origin = spot.at(-sign * (step - 1))
            if step < half_way:
                first, count = 0, tile
            else:
                first, count = way * (tile // 2), tile // 2
            src = own.at[pl.ds(first, count), :] if step == 1 else view(origin, first, count)
            copy = remote(
                src,
                view(origin, first, count),
                sends.at[item, step - 1, way],
                recvs.at[item, step - 1, way],
                target,
            )
            if only is None:
                pair.append((copy, None, None))
            else:
                pair.append((copy, origin == only, spot.at(-sign * step) == only))
        steps.append(pair)
    return steps


def when(cond, body):
    if cond is None:
        body()
    else:
        pl.when(cond)(body)


def start_pair(pair):
    for copy, sent, _ in pair:
        when(sent, copy.start)


def pair_arrives(pair):
    for copy, _, arrives in pair:
        when(arrives, copy.wait_recv)


def pair_left(pair):
    for copy, sent, _ in pair:
        when(sent, copy.wait_send)


def pass_on(steps):
    for step in range(1, len(steps)):
        pair_arrives(steps[step - 1])
        start_pair(steps[step])


def gather_kernel(
    rows, cols, x_ref, g_ref, xr, xh, gr, gh, gc, xs, gs, zs, zr, rs, rr, ss, sr, ls, *symmetric
):
    spot = Spot(rows, cols)
    height, width = x_ref.shape
    c, l = spot.c, spot.l

    def wide(ref, col):
        return ref.at[:, pl.ds(pl.multiple_of((col * 2 + l) * width, width), width)]

    def x_view(col):
        def view(row, first, count):
            return xh.at[
                pl.ds(pl.multiple_of(row * height + first, 16), count),
                pl.ds(pl.multiple_of(col * width, width), width),
            ]

        return view

    def g_view(row, first, count):
        return gc.at[pl.ds(pl.multiple_of(row * height + first, 16), count), :]

    def slot(kind, col):
        return (xs, gs)[kind].at[col]

    def tile_of(kind, item):
        if item[1] == 0:
            return (x_ref, g_ref)[kind]
        return slot(kind, col_of(item))

    spot.greet((spot.right, spot.left, spot.sibling, spot.up, spot.down))

    items = [(0, 0)] + [(way, d) for d in range(1, cols) for way in (0, 1)]
    index_of = {item: i for i, item in enumerate(items)}

    def col_of(item):
        way, d = item
        return c - d if way == 0 else c + d

    def there(item):
        way, d = item
        if d == 0:
            return None
        return c >= d if way == 0 else c < cols - d

    def both(a, b):
        return b if a is None else jnp.logical_and(a, b)

    def line_copy(kind, way, d):
        col = c - d if way == 0 else c + d
        src = tile_of(kind, (way, d))
        target = spot.up if way == 0 else spot.down
        return remote(src, slot(kind, col), zs.at[kind, way, d], zr.at[kind, way, d], target)

    def line_sends(way, d):
        further = c < cols - 1 if way == 0 else c > 0
        return both(there((way, d)), further)

    def sibling_copy(kind, item):
        i = index_of[item]
        dst = wide((xr, gr)[kind], col_of(item))
        return remote(tile_of(kind, item), dst, ss.at[kind, i], sr.at[kind, i], spot.sibling)

    def local_copies(kind, item):
        i = index_of[item]
        col = col_of(item)
        src = tile_of(kind, item)
        if kind == 0:
            targets = (wide(xr, col), x_view(col)(spot.r, 0, height))
        else:
            targets = (wide(gr, col), gh.at[:, pl.ds(pl.multiple_of(col * width, width), width)])
        return [pltpu.make_async_copy(src, dst, ls.at[kind, j, i]) for j, dst in enumerate(targets)]

    if symmetric:
        rb, eb, tb, es, er, ts, tr, dl = symmetric

    def sent_half(row, col):
        return l + (row < col).astype(jnp.int32) * (1 - 2 * l)

    def rows_at(tile, half):
        return tile.at[pl.ds(pl.multiple_of(half * width, width), width), :]

    def x_rings(item):
        i, col, tile = index_of[item], col_of(item), tile_of(0, item)
        if not symmetric:
            return [ring_copies(spot, x_view(col), tile, rs, rr, i)]

        def view(row, first, count):
            return rb.at[row, col, pl.ds(first, count), :]

        def extra_view(row, first, count):
            return eb.at[col, pl.ds(first, count), :]

        half = sent_half(spot.r, col)
        return [
            ring_copies(spot, view, rows_at(tile, half), rs, rr, i),
            ring_copies(spot, extra_view, rows_at(tile, 1 - half), es, er, i, only=col),
        ]

    def x_start(item):
        for steps in x_rings(item):
            start_pair(steps[0])

    def turned(item, offset, row):
        i, col = index_of[item], col_of(item)
        src = tb.at[row, col]
        dst = xh.at[
            pl.ds(pl.multiple_of(col * height + l * width, width), width),
            pl.ds(pl.multiple_of(row * width, width), width),
        ]
        return (
            pltpu.make_async_copy(src, dst, dl.at[1, offset, i]),
            remote(src, dst, ts.at[offset, i], tr.at[offset, i], spot.sibling),
        )

    def placed(item, offset, row):
        i, col = index_of[item], col_of(item)
        half = sent_half(row, col)

        def target(h):
            return x_view(col)(row, h * width, width)

        return (
            pltpu.make_async_copy(rb.at[row, col], target(half), dl.at[0, offset, i]),
            pltpu.make_async_copy(eb.at[col], target(1 - half), dl.at[2, 0, i]),
        )

    def turn(item, offset, row, src):
        col = col_of(item)

        @pl.when(jnp.logical_and(row != col, col != spot.r))
        def _():
            @pl.loop(0, width // BS)
            def _(strip):
                at = pl.ds(pl.multiple_of(strip * BS, BS), BS)
                tb[row, col, at, :] = src[:, at].T

            here, there_ = turned(item, offset, row)
            pl.when(row > col)(here.start)
            pl.when(row < col)(there_.start)

    def turn_done(item, offset, row):
        col = col_of(item)

        @pl.when(jnp.logical_and(row != col, col != spot.r))
        def _():
            here, there_ = turned(item, offset, row)
            pl.when(row > col)(here.wait)
            pl.when(row < col)(there_.wait)

    def turn_own(item):
        if symmetric:
            half = sent_half(spot.r, col_of(item))
            turn(item, 0, spot.r, rows_at(tile_of(0, item), half))

    def take(item):
        for steps in x_rings(item):
            pair_arrives(steps[-1])
        if symmetric:

            @pl.loop(1, rows)
            def _(offset):
                row = spot.at(offset)
                tile, extra = placed(item, offset, row)
                tile.start()
                pl.when(row == col_of(item))(extra.start)
                turn(item, offset, row, rb.at[row, col_of(item)])

    def take_done(item):
        if symmetric:
            turn_done(item, 0, spot.r)

            @pl.loop(1, rows)
            def _(offset):
                row = spot.at(offset)
                tile, extra = placed(item, offset, row)
                tile.wait()
                pl.when(row == col_of(item))(extra.wait)
                turn_done(item, offset, row)

    g_item = len(items)

    def g_ring():
        return ring_copies(spot, g_view, g_ref, rs, rr, g_item)

    def g_col_copy():
        return pltpu.make_async_copy(g_ref, g_view(spot.r, 0, height), ls.at[0, 0, len(items)])

    def spread(kind, item):
        sibling_copy(kind, item).start()
        for copy in local_copies(kind, item):
            copy.start()

    for way in (0, 1):
        when(line_sends(way, 0), lambda way=way: line_copy(0, way, 0).start())
    x_start((0, 0))
    start_pair(g_ring()[0])
    g_col_copy().start()
    for kind in (0, 1):
        spread(kind, (0, 0))

    def line_g_start(way, d):
        last = (c if way == 0 else cols - 1 - c) == d
        when(both(line_sends(way, 0), last), line_copy(1, way, 0).start)

    for way in (0, 1):
        line_g_start(way, 0)

    def arrive_x(item):
        way, d = item
        line_copy(0, way, d - 1).wait_recv()
        when(line_sends(way, d) if d < cols - 1 else jnp.bool_(False), lambda: line_copy(0, way, d).start())
        line_g_start(way, d)
        x_start(item)
        spread(0, item)

    def arrive_g(item):
        way, d = item
        line_copy(1, way, d - 1).wait_recv()
        when(line_sends(way, d) if d < cols - 1 else jnp.bool_(False), lambda: line_copy(1, way, d).start())
        spread(1, item)

    def ring_on(item):
        for steps in x_rings(item):
            pass_on(steps)

    turn_own((0, 0))
    previous = [(0, 0)]
    def each(some, body):
        for item in some:
            when(there(item), lambda item=item: body(item))

    for d in range(1, cols):
        current = [(0, d), (1, d)]
        each(current, arrive_x)
        each(previous, ring_on)
        if d == 1:
            pass_on(g_ring())
        each(current, turn_own)
        each(previous, take)
        previous = current
    each([(0, 1), (1, 1)], arrive_g)
    each(previous, ring_on)
    for d in range(2, cols):
        each([(0, d), (1, d)], arrive_g)
        if d == 2:
            each(previous, take)
    if cols < 3:
        each(previous, take)

    def finish(item):
        way, d = item
        for steps in x_rings(item):
            for pair in steps:
                pair_left(pair)
        take_done(item)
        for kind in (0, 1):
            copy = sibling_copy(kind, item)
            copy.wait_send()
            copy.wait_recv()
            for copy in local_copies(kind, item):
                copy.wait()

    each(items, finish)
    steps = g_ring()
    for pair in steps:
        pair_left(pair)
    pair_arrives(steps[-1])
    g_col_copy().wait()
    for kind in (0, 1):
        for way in (0, 1):
            for d in range(cols - 1):
                when(line_sends(way, d), lambda kind=kind, way=way, d=d: line_copy(kind, way, d).wait_send())


def share_kernel(rows, cols, width, s_ref, p_ref, sf, pf, pc, rs, rr, ss, sr, ls):
    spot = Spot(rows, cols)
    height = s_ref.shape[0]
    spot.greet((spot.right, spot.left, spot.sibling))
    mine = p_ref.at[:, pl.ds(pl.multiple_of(spot.c * width, width), width)]

    def view(row, first, count):
        return pc.at[pl.ds(pl.multiple_of(row * height + first, 16), count), :]

    steps = ring_copies(spot, view, mine, rs, rr, 0)
    start_pair(steps[0])
    others = [pltpu.make_async_copy(mine, view(spot.r, 0, height), ls.at[2 * cols])]
    for kind, (half, full) in enumerate(((p_ref, pf), (s_ref, sf))):
        for col in range(cols):
            src = half.at[:, pl.ds(col * width, width)]
            dst = full.at[:, pl.ds(pl.multiple_of((col * 2 + spot.l) * width, width), width)]
            others.append(remote(src, dst, ss.at[kind, col], sr.at[kind, col], spot.sibling))
            others.append(pltpu.make_async_copy(src, dst, ls.at[kind * cols + col]))
    for copy in others:
        copy.start()
    pass_on(steps)
    pair_arrives(steps[-1])
    for pair in steps:
        pair_left(pair)
    for copy in others:
        copy.wait()


def gather_all(rows, cols, x, g):
    height, width = x.shape
    shape = lambda a, b: jax.ShapeDtypeStruct((a, b), x.dtype)
    items = 2 * cols - 1
    dma = pltpu.SemaphoreType.DMA
    symmetric = []
    if height == 2 * width and rows == cols:
        symmetric = [
            pltpu.VMEM((rows, cols, width, width), x.dtype),
            pltpu.VMEM((cols, width, width), x.dtype),
            pltpu.VMEM((rows, cols, width, width), x.dtype),
            dma((items, rows // 2, 2)),
            dma((items, rows // 2, 2)),
            dma((rows, items)),
            dma((rows, items)),
            dma((3, rows, items)),
        ]
    return pl.pallas_call(
        lambda *refs: gather_kernel(rows, cols, *refs),
        out_shape=(
            shape(height, 2 * cols * width),
            shape(rows * height, cols * width),
            shape(height, 2 * cols * width),
            shape(height, cols * width),
            shape(rows * height, width),
        ),
        in_specs=[VMEM] * 2,
        out_specs=(ANY,) * 5,
        scratch_shapes=[
            pltpu.VMEM((cols, height, width), x.dtype),
            pltpu.VMEM((cols, height, width), x.dtype),
            dma((2, 2, cols)),
            dma((2, 2, cols)),
            dma((items + 1, rows // 2, 2)),
            dma((items + 1, rows // 2, 2)),
            dma((2, items)),
            dma((2, items)),
            dma((2, 2, items + 1)),
            *symmetric,
        ],
        compiler_params=pltpu.CompilerParams(collective_id=0, has_side_effects=True, vmem_limit_bytes=VMEM_LIMIT),
        name="gather_all",
    )(x, g)


def share(rows, cols, width, s, p):
    height = s.shape[0]
    shape = lambda a, b: jax.ShapeDtypeStruct((a, b), s.dtype)
    dma = pltpu.SemaphoreType.DMA
    return pl.pallas_call(
        lambda *refs: share_kernel(rows, cols, width, *refs),
        out_shape=(
            shape(height, 2 * cols * width),
            shape(height, 2 * cols * width),
            shape(rows * height, width),
        ),
        in_specs=[VMEM] * 2,
        out_specs=(ANY,) * 3,
        scratch_shapes=[
            dma((1, rows // 2, 2)),
            dma((1, rows // 2, 2)),
            dma((2, cols)),
            dma((2, cols)),
            dma((2 * cols + 1,)),
        ],
        compiler_params=pltpu.CompilerParams(collective_id=1, has_side_effects=True, vmem_limit_bytes=VMEM_LIMIT),
        name="share",
    )(s, p)


def dot(a, b):
    return jnp.dot(a, b, preferred_element_type=jnp.float32)


def hits(blocks, positions):
    return (blocks[:, None] == positions[None, :] // BS).astype(jnp.bfloat16)


def mask_of(block_pattern, row_positions, col_positions):
    counted = jnp.einsum(
        "nr,nc->rc",
        hits(block_pattern[0], row_positions),
        hits(block_pattern[1], col_positions),
        preferred_element_type=jnp.float32,
    )
    return counted > 0.5


def solution(mesh):
    rows, cols, layers = mesh.shape["row"], mesh.shape["col"], mesh.shape["layer"]

    def per_device(density, cotangent, block_pattern):
        height, width = density.shape
        r, c, l = (lax.axis_index(name) for name in ("row", "col", "layer"))
        row_at = r * height + jnp.arange(height, dtype=jnp.int32)
        col_at = (c * layers + l) * width + jnp.arange(width, dtype=jnp.int32)
        along = jnp.arange(cols * width, dtype=jnp.int32)
        half_at = ((along // width) * layers + l) * width + along % width
        mask = mask_of(block_pattern, row_at, col_at)
        half_mask = mask_of(block_pattern, row_at, half_at)
        xm = jnp.where(mask, density, jnp.zeros_like(density))
        masked_grad = jnp.where(mask, cotangent, jnp.zeros_like(cotangent))
        x_rows, x_half, g_rows, g_half, g_cols = gather_all(rows, cols, xm, masked_grad)
        square = jnp.where(half_mask, dot(x_rows, x_half), 0.0).astype(jnp.bfloat16)
        pulled = jnp.where(
            half_mask, 3.0 * g_half.astype(jnp.float32) - 2.0 * dot(g_rows, x_half), 0.0
        ).astype(jnp.bfloat16)
        s_rows, p_rows, p_cols = share(rows, cols, width, square, pulled)
        x_cols = lax.dynamic_slice_in_dim(x_half, c * width, width, axis=1)
        total = -2.0 * dot(s_rows, g_cols) + dot(p_rows, x_cols) + dot(x_rows, p_cols)
        return jnp.where(mask, total, 0.0)

    return jax.shard_map(
        per_device,
        mesh=mesh,
        in_specs=(P("row", ("col", "layer")), P("row", ("col", "layer")), P()),
        out_specs=P("row", ("col", "layer")),
        check_vma=False,
    )
```

```python
import jax
import jax.numpy as jnp
from jax import lax
from jax.experimental import pallas as pl
from jax.experimental.pallas import tpu as pltpu
from jax.sharding import PartitionSpec as P

BS = 128
MESH = pl.DeviceIdType.MESH
ANY = pl.BlockSpec(memory_space=pl.ANY)
VMEM = pl.BlockSpec(memory_space=pltpu.VMEM)
VMEM_LIMIT = 48 * 2**20


def ring_place(index, size):
    upper = index // (size // 2)
    return index + upper * (size + size // 2 - 1 - 2 * index)


class Spot:
    def __init__(self, rows, cols):
        self.rows, self.cols = rows, cols
        self.r = lax.axis_index("row")
        self.c = lax.axis_index("col")
        self.l = lax.axis_index("layer")
        self.p = ring_place(self.r, rows)
        self.right = (self.at(1), self.c, self.l)
        self.left = (self.at(-1), self.c, self.l)
        self.sibling = (self.r, self.c, 1 - self.l)
        self.up = (self.r, lax.rem(self.c + 1, cols), self.l)
        self.down = (self.r, lax.rem(self.c + cols - 1, cols), self.l)

    def at(self, step):
        return ring_place(lax.rem(self.p + step + self.rows, self.rows), self.rows)

    def greet(self, others):
        barrier = pltpu.get_barrier_semaphore()
        for other in others:
            pl.semaphore_signal(barrier, inc=1, device_id=other, device_id_type=MESH)
        pl.semaphore_wait(barrier, len(others))


def remote(src, dst, send, recv, device):
    return pltpu.make_async_remote_copy(
        src_ref=src, dst_ref=dst, send_sem=send, recv_sem=recv, device_id=device, device_id_type=MESH
    )


def ring_copies(spot, view, own, sends, recvs, item, only=None):
    half_way = spot.rows // 2
    tile = own.shape[0]
    steps = []
    for step in range(1, half_way + 1):
        pair = []
        for way, (target, sign) in enumerate(((spot.right, 1), (spot.left, -1))):
            origin = spot.at(-sign * (step - 1))
            if step < half_way:
                first, count = 0, tile
            else:
                first, count = way * (tile // 2), tile // 2
            src = own.at[pl.ds(first, count), :] if step == 1 else view(origin, first, count)
            copy = remote(
                src,
                view(origin, first, count),
                sends.at[item, step - 1, way],
                recvs.at[item, step - 1, way],
                target,
            )
            if only is None:
                pair.append((copy, None, None))
            else:
                pair.append((copy, origin == only, spot.at(-sign * step) == only))
        steps.append(pair)
    return steps


def when(cond, body):
    if cond is None:
        body()
    else:
        pl.when(cond)(body)


def start_pair(pair):
    for copy, sent, _ in pair:
        when(sent, copy.start)


def pair_arrives(pair):
    for copy, _, arrives in pair:
        when(arrives, copy.wait_recv)


def pair_left(pair):
    for copy, sent, _ in pair:
        when(sent, copy.wait_send)


def pass_on(steps):
    for step in range(1, len(steps)):
        pair_arrives(steps[step - 1])
        start_pair(steps[step])


def gather_kernel(
    rows, cols, x_ref, g_ref, xr, xh, gr, gh, gc, xs, gs, zs, zr, rs, rr, ss, sr, ls, *symmetric
):
    spot = Spot(rows, cols)
    height, width = x_ref.shape
    c, l = spot.c, spot.l

    def wide(ref, col):
        return ref.at[:, pl.ds(pl.multiple_of((col * 2 + l) * width, width), width)]

    def x_view(col):
        def view(row, first, count):
            return xh.at[
                pl.ds(pl.multiple_of(row * height + first, 16), count),
                pl.ds(pl.multiple_of(col * width, width), width),
            ]

        return view

    def g_view(row, first, count):
        return gc.at[pl.ds(pl.multiple_of(row * height + first, 16), count), :]

    def slot(kind, col):
        return (xs, gs)[kind].at[col]

    def tile_of(kind, item):
        if item[1] == 0:
            return (x_ref, g_ref)[kind]
        return slot(kind, col_of(item))

    spot.greet((spot.right, spot.left, spot.sibling, spot.up, spot.down))

    items = [(0, 0)] + [(way, d) for d in range(1, cols) for way in (0, 1)]
    index_of = {item: i for i, item in enumerate(items)}

    def col_of(item):
        way, d = item
        return c - d if way == 0 else c + d

    def there(item):
        way, d = item
        if d == 0:
            return None
        return c >= d if way == 0 else c < cols - d

    def both(a, b):
        return b if a is None else jnp.logical_and(a, b)

    def line_copy(kind, way, d):
        col = c - d if way == 0 else c + d
        src = tile_of(kind, (way, d))
        target = spot.up if way == 0 else spot.down
        return remote(src, slot(kind, col), zs.at[kind, way, d], zr.at[kind, way, d], target)

    def line_sends(way, d):
        further = c < cols - 1 if way == 0 else c > 0
        return both(there((way, d)), further)

    def sibling_copy(kind, item):
        i = index_of[item]
        dst = wide((xr, gr)[kind], col_of(item))
        return remote(tile_of(kind, item), dst, ss.at[kind, i], sr.at[kind, i], spot.sibling)

    def local_copies(kind, item):
        i = index_of[item]
        col = col_of(item)
        src = tile_of(kind, item)
        if kind == 0:
            targets = (wide(xr, col), x_view(col)(spot.r, 0, height))
        else:
            targets = (wide(gr, col), gh.at[:, pl.ds(pl.multiple_of(col * width, width), width)])
        return [pltpu.make_async_copy(src, dst, ls.at[kind, j, i]) for j, dst in enumerate(targets)]

    if symmetric:
        rb, eb, tb, es, er, ts, tr, dl = symmetric

    def sent_half(row, col):
        return l + (row < col).astype(jnp.int32) * (1 - 2 * l)

    def rows_at(tile, half):
        return tile.at[pl.ds(pl.multiple_of(half * width, width), width), :]

    def x_rings(item):
        i, col, tile = index_of[item], col_of(item), tile_of(0, item)
        if not symmetric:
            return [ring_copies(spot, x_view(col), tile, rs, rr, i)]

        def view(row, first, count):
            return rb.at[row, col, pl.ds(first, count), :]

        def extra_view(row, first, count):
            return eb.at[col, pl.ds(first, count), :]

        half = sent_half(spot.r, col)
        return [
            ring_copies(spot, view, rows_at(tile, half), rs, rr, i),
            ring_copies(spot, extra_view, rows_at(tile, 1 - half), es, er, i, only=col),
        ]

    def x_start(item):
        for steps in x_rings(item):
            start_pair(steps[0])

    def turned(item, offset, row):
        i, col = index_of[item], col_of(item)
        src = tb.at[row, col]
        dst = xh.at[
            pl.ds(pl.multiple_of(col * height + l * width, width), width),
            pl.ds(pl.multiple_of(row * width, width), width),
        ]
        return (
            pltpu.make_async_copy(src, dst, dl.at[1, offset, i]),
            remote(src, dst, ts.at[offset, i], tr.at[offset, i], spot.sibling),
        )

    def placed(item, offset, row):
        i, col = index_of[item], col_of(item)
        half = sent_half(row, col)

        def target(h):
            return x_view(col)(row, h * width, width)

        return (
            pltpu.make_async_copy(rb.at[row, col], target(half), dl.at[0, offset, i]),
            pltpu.make_async_copy(eb.at[col], target(1 - half), dl.at[2, 0, i]),
        )

    def turn(item, offset, row, src):
        col = col_of(item)

        @pl.when(jnp.logical_and(row != col, col != spot.r))
        def _():
            @pl.loop(0, width // BS)
            def _(strip):
                at = pl.ds(pl.multiple_of(strip * BS, BS), BS)
                tb[row, col, at, :] = src[:, at].T

            here, there_ = turned(item, offset, row)
            pl.when(row > col)(here.start)
            pl.when(row < col)(there_.start)

    def turn_done(item, offset, row):
        col = col_of(item)

        @pl.when(jnp.logical_and(row != col, col != spot.r))
        def _():
            here, there_ = turned(item, offset, row)
            pl.when(row > col)(here.wait)
            pl.when(row < col)(there_.wait)

    def turn_own(item):
        if symmetric:
            half = sent_half(spot.r, col_of(item))
            turn(item, 0, spot.r, rows_at(tile_of(0, item), half))

    def take(item):
        for steps in x_rings(item):
            pair_arrives(steps[-1])
        if symmetric:

            @pl.loop(1, rows)
            def _(offset):
                row = spot.at(offset)
                tile, extra = placed(item, offset, row)
                tile.start()
                pl.when(row == col_of(item))(extra.start)
                turn(item, offset, row, rb.at[row, col_of(item)])

    def take_done(item):
        if symmetric:
            turn_done(item, 0, spot.r)

            @pl.loop(1, rows)
            def _(offset):
                row = spot.at(offset)
                tile, extra = placed(item, offset, row)
                tile.wait()
                pl.when(row == col_of(item))(extra.wait)
                turn_done(item, offset, row)

    g_item = len(items)

    def g_ring():
        return ring_copies(spot, g_view, g_ref, rs, rr, g_item)

    def g_col_copy():
        return pltpu.make_async_copy(g_ref, g_view(spot.r, 0, height), ls.at[0, 0, len(items)])

    def spread(kind, item):
        sibling_copy(kind, item).start()
        for copy in local_copies(kind, item):
            copy.start()

    for way in (0, 1):
        when(line_sends(way, 0), lambda way=way: line_copy(0, way, 0).start())
    x_start((0, 0))
    start_pair(g_ring()[0])
    g_col_copy().start()
    for kind in (0, 1):
        spread(kind, (0, 0))
    def arrive_x(item):
        way, d = item
        line_copy(0, way, d - 1).wait_recv()
        when(line_sends(way, d) if d < cols - 1 else jnp.bool_(False), lambda: line_copy(0, way, d).start())
        x_start(item)
        spread(0, item)

    def arrive_g(item):
        way, d = item
        line_copy(1, way, d - 1).wait_recv()
        when(line_sends(way, d) if d < cols - 1 else jnp.bool_(False), lambda: line_copy(1, way, d).start())
        spread(1, item)

    def ring_on(item):
        for steps in x_rings(item):
            pass_on(steps)

    turn_own((0, 0))
    previous = [(0, 0)]
    def each(some, body):
        for item in some:
            when(there(item), lambda item=item: body(item))

    for d in range(1, cols):
        current = [(0, d), (1, d)]
        each(current, arrive_x)
        if d == 1:
            for way in (0, 1):
                when(line_sends(way, 0), line_copy(1, way, 0).start)
        else:
            each([(0, d - 1), (1, d - 1)], arrive_g)
        each(previous, ring_on)
        if d == 1:
            pass_on(g_ring())
        each(current, turn_own)
        each(previous, take)
        previous = current
    each(previous, ring_on)
    each(previous, take)
    each(previous, arrive_g)

    def finish(item):
        way, d = item
        for steps in x_rings(item):
            for pair in steps:
                pair_left(pair)
        take_done(item)
        for kind in (0, 1):
            copy = sibling_copy(kind, item)
            copy.wait_send()
            copy.wait_recv()
            for copy in local_copies(kind, item):
                copy.wait()

    each(items, finish)
    steps = g_ring()
    for pair in steps:
        pair_left(pair)
    pair_arrives(steps[-1])
    g_col_copy().wait()
    for kind in (0, 1):
        for way in (0, 1):
            for d in range(cols - 1):
                when(line_sends(way, d), lambda kind=kind, way=way, d=d: line_copy(kind, way, d).wait_send())


def share_kernel(rows, cols, width, s_ref, p_ref, sf, pf, pc, rs, rr, ss, sr, ls):
    spot = Spot(rows, cols)
    height = s_ref.shape[0]
    spot.greet((spot.right, spot.left, spot.sibling))
    mine = p_ref.at[:, pl.ds(pl.multiple_of(spot.c * width, width), width)]

    def view(row, first, count):
        return pc.at[pl.ds(pl.multiple_of(row * height + first, 16), count), :]

    steps = ring_copies(spot, view, mine, rs, rr, 0)
    start_pair(steps[0])
    others = [pltpu.make_async_copy(mine, view(spot.r, 0, height), ls.at[2 * cols])]
    for kind, (half, full) in enumerate(((p_ref, pf), (s_ref, sf))):
        for col in range(cols):
            src = half.at[:, pl.ds(col * width, width)]
            dst = full.at[:, pl.ds(pl.multiple_of((col * 2 + spot.l) * width, width), width)]
            others.append(remote(src, dst, ss.at[kind, col], sr.at[kind, col], spot.sibling))
            others.append(pltpu.make_async_copy(src, dst, ls.at[kind * cols + col]))
    for copy in others:
        copy.start()
    pass_on(steps)
    pair_arrives(steps[-1])
    for pair in steps:
        pair_left(pair)
    for copy in others:
        copy.wait()


def gather_all(rows, cols, x, g):
    height, width = x.shape
    shape = lambda a, b: jax.ShapeDtypeStruct((a, b), x.dtype)
    items = 2 * cols - 1
    dma = pltpu.SemaphoreType.DMA
    symmetric = []
    if height == 2 * width and rows == cols:
        symmetric = [
            pltpu.VMEM((rows, cols, width, width), x.dtype),
            pltpu.VMEM((cols, width, width), x.dtype),
            pltpu.VMEM((rows, cols, width, width), x.dtype),
            dma((items, rows // 2, 2)),
            dma((items, rows // 2, 2)),
            dma((rows, items)),
            dma((rows, items)),
            dma((3, rows, items)),
        ]
    return pl.pallas_call(
        lambda *refs: gather_kernel(rows, cols, *refs),
        out_shape=(
            shape(height, 2 * cols * width),
            shape(rows * height, cols * width),
            shape(height, 2 * cols * width),
            shape(height, cols * width),
            shape(rows * height, width),
        ),
        in_specs=[VMEM] * 2,
        out_specs=(ANY,) * 5,
        scratch_shapes=[
            pltpu.VMEM((cols, height, width), x.dtype),
            pltpu.VMEM((cols, height, width), x.dtype),
            dma((2, 2, cols)),
            dma((2, 2, cols)),
            dma((items + 1, rows // 2, 2)),
            dma((items + 1, rows // 2, 2)),
            dma((2, items)),
            dma((2, items)),
            dma((2, 2, items + 1)),
            *symmetric,
        ],
        compiler_params=pltpu.CompilerParams(collective_id=0, has_side_effects=True, vmem_limit_bytes=VMEM_LIMIT),
        name="gather_all",
    )(x, g)


def share(rows, cols, width, s, p):
    height = s.shape[0]
    shape = lambda a, b: jax.ShapeDtypeStruct((a, b), s.dtype)
    dma = pltpu.SemaphoreType.DMA
    return pl.pallas_call(
        lambda *refs: share_kernel(rows, cols, width, *refs),
        out_shape=(
            shape(height, 2 * cols * width),
            shape(height, 2 * cols * width),
            shape(rows * height, width),
        ),
        in_specs=[VMEM] * 2,
        out_specs=(ANY,) * 3,
        scratch_shapes=[
            dma((1, rows // 2, 2)),
            dma((1, rows // 2, 2)),
            dma((2, cols)),
            dma((2, cols)),
            dma((2 * cols + 1,)),
        ],
        compiler_params=pltpu.CompilerParams(collective_id=1, has_side_effects=True, vmem_limit_bytes=VMEM_LIMIT),
        name="share",
    )(s, p)


def dot(a, b):
    return jnp.dot(a, b, preferred_element_type=jnp.float32)


def hits(blocks, positions):
    return (blocks[:, None] == positions[None, :] // BS).astype(jnp.bfloat16)


def mask_of(block_pattern, row_positions, col_positions):
    counted = jnp.einsum(
        "nr,nc->rc",
        hits(block_pattern[0], row_positions),
        hits(block_pattern[1], col_positions),
        preferred_element_type=jnp.float32,
    )
    return counted > 0.5


def solution(mesh):
    rows, cols, layers = mesh.shape["row"], mesh.shape["col"], mesh.shape["layer"]

    def per_device(density, cotangent, block_pattern):
        height, width = density.shape
        r, c, l = (lax.axis_index(name) for name in ("row", "col", "layer"))
        row_at = r * height + jnp.arange(height, dtype=jnp.int32)
        col_at = (c * layers + l) * width + jnp.arange(width, dtype=jnp.int32)
        along = jnp.arange(cols * width, dtype=jnp.int32)
        half_at = ((along // width) * layers + l) * width + along % width
        mask = mask_of(block_pattern, row_at, col_at)
        half_mask = mask_of(block_pattern, row_at, half_at)
        xm = jnp.where(mask, density, jnp.zeros_like(density))
        masked_grad = jnp.where(mask, cotangent, jnp.zeros_like(cotangent))
        x_rows, x_half, g_rows, g_half, g_cols = gather_all(rows, cols, xm, masked_grad)
        square = jnp.where(half_mask, dot(x_rows, x_half), 0.0).astype(jnp.bfloat16)
        pulled = jnp.where(
            half_mask, 3.0 * g_half.astype(jnp.float32) - 2.0 * dot(g_rows, x_half), 0.0
        ).astype(jnp.bfloat16)
        s_rows, p_rows, p_cols = share(rows, cols, width, square, pulled)
        x_cols = lax.dynamic_slice_in_dim(x_half, c * width, width, axis=1)
        total = -2.0 * dot(s_rows, g_cols) + dot(p_rows, x_cols) + dot(x_rows, p_cols)
        return jnp.where(mask, total, 0.0)

    return jax.shard_map(
        per_device,
        mesh=mesh,
        in_specs=(P("row", ("col", "layer")), P("row", ("col", "layer")), P()),
        out_specs=P("row", ("col", "layer")),
        check_vma=False,
    )
```

```python
import jax
import jax.numpy as jnp
from jax import lax
from jax.experimental import pallas as pl
from jax.experimental.pallas import tpu as pltpu
from jax.sharding import PartitionSpec as P

BS = 128
MESH = pl.DeviceIdType.MESH
ANY = pl.BlockSpec(memory_space=pl.ANY)
VMEM = pl.BlockSpec(memory_space=pltpu.VMEM)
VMEM_LIMIT = 48 * 2**20


def ring_place(index, size):
    upper = index // (size // 2)
    return index + upper * (size + size // 2 - 1 - 2 * index)


class Spot:
    def __init__(self, rows, cols):
        self.rows, self.cols = rows, cols
        self.r = lax.axis_index("row")
        self.c = lax.axis_index("col")
        self.l = lax.axis_index("layer")
        self.p = ring_place(self.r, rows)
        self.right = (self.at(1), self.c, self.l)
        self.left = (self.at(-1), self.c, self.l)
        self.sibling = (self.r, self.c, 1 - self.l)
        self.up = (self.r, lax.rem(self.c + 1, cols), self.l)
        self.down = (self.r, lax.rem(self.c + cols - 1, cols), self.l)

    def at(self, step):
        return ring_place(lax.rem(self.p + step + self.rows, self.rows), self.rows)

    def greet(self, others):
        barrier = pltpu.get_barrier_semaphore()
        for other in others:
            pl.semaphore_signal(barrier, inc=1, device_id=other, device_id_type=MESH)
        pl.semaphore_wait(barrier, len(others))


def remote(src, dst, send, recv, device):
    return pltpu.make_async_remote_copy(
        src_ref=src, dst_ref=dst, send_sem=send, recv_sem=recv, device_id=device, device_id_type=MESH
    )


def ring_copies(spot, view, own, sends, recvs, item, only=None):
    half_way = spot.rows // 2
    tile = own.shape[0]
    steps = []
    for step in range(1, half_way + 1):
        pair = []
        for way, (target, sign) in enumerate(((spot.right, 1), (spot.left, -1))):
            origin = spot.at(-sign * (step - 1))
            if step < half_way:
                first, count = 0, tile
            else:
                first, count = way * (tile // 2), tile // 2
            src = own.at[pl.ds(first, count), :] if step == 1 else view(origin, first, count)
            copy = remote(
                src,
                view(origin, first, count),
                sends.at[item, step - 1, way],
                recvs.at[item, step - 1, way],
                target,
            )
            if only is None:
                pair.append((copy, None, None))
            else:
                pair.append((copy, origin == only, spot.at(-sign * step) == only))
        steps.append(pair)
    return steps


def when(cond, body):
    if cond is None:
        body()
    else:
        pl.when(cond)(body)


def start_pair(pair):
    for copy, sent, _ in pair:
        when(sent, copy.start)


def pair_arrives(pair):
    for copy, _, arrives in pair:
        when(arrives, copy.wait_recv)


def pair_left(pair):
    for copy, sent, _ in pair:
        when(sent, copy.wait_send)


def pass_on(steps):
    for step in range(1, len(steps)):
        pair_arrives(steps[step - 1])
        start_pair(steps[step])


def gather_kernel(
    rows, cols, x_ref, g_ref, xr, xh, gr, gh, gc, xs, gs, zs, zr, rs, rr, ss, sr, ls, *symmetric
):
    spot = Spot(rows, cols)
    height, width = x_ref.shape
    c, l = spot.c, spot.l

    def wide(ref, col):
        return ref.at[:, pl.ds(pl.multiple_of((col * 2 + l) * width, width), width)]

    def x_view(col):
        def view(row, first, count):
            return xh.at[
                pl.ds(pl.multiple_of(row * height + first, 16), count),
                pl.ds(pl.multiple_of(col * width, width), width),
            ]

        return view

    def g_view(row, first, count):
        return gc.at[pl.ds(pl.multiple_of(row * height + first, 16), count), :]

    def slot(kind, col):
        return (xs, gs)[kind].at[col]

    def tile_of(kind, item):
        if item[1] == 0:
            return (x_ref, g_ref)[kind]
        return slot(kind, col_of(item))

    spot.greet((spot.right, spot.left, spot.sibling, spot.up, spot.down))

    items = [(0, 0)] + [(way, d) for d in range(1, cols) for way in (0, 1)]
    index_of = {item: i for i, item in enumerate(items)}

    def col_of(item):
        way, d = item
        return c - d if way == 0 else c + d

    def there(item):
        way, d = item
        if d == 0:
            return None
        return c >= d if way == 0 else c < cols - d

    def both(a, b):
        return b if a is None else jnp.logical_and(a, b)

    def line_copy(kind, way, d):
        col = c - d if way == 0 else c + d
        src = tile_of(kind, (way, d))
        target = spot.up if way == 0 else spot.down
        return remote(src, slot(kind, col), zs.at[kind, way, d], zr.at[kind, way, d], target)

    def line_sends(way, d):
        further = c < cols - 1 if way == 0 else c > 0
        return both(there((way, d)), further)

    def sibling_copy(kind, item):
        i = index_of[item]
        dst = wide((xr, gr)[kind], col_of(item))
        return remote(tile_of(kind, item), dst, ss.at[kind, i], sr.at[kind, i], spot.sibling)

    def local_copies(kind, item):
        i = index_of[item]
        col = col_of(item)
        src = tile_of(kind, item)
        if kind == 0:
            targets = (wide(xr, col), x_view(col)(spot.r, 0, height))
        else:
            targets = (wide(gr, col), gh.at[:, pl.ds(pl.multiple_of(col * width, width), width)])
        return [pltpu.make_async_copy(src, dst, ls.at[kind, j, i]) for j, dst in enumerate(targets)]

    if symmetric:
        rb, eb, tb, es, er, ts, tr, dl = symmetric

    def sent_half(row, col):
        return l + (row < col).astype(jnp.int32) * (1 - 2 * l)

    def rows_at(tile, half):
        return tile.at[pl.ds(pl.multiple_of(half * width, width), width), :]

    def x_rings(item):
        i, col, tile = index_of[item], col_of(item), tile_of(0, item)
        if not symmetric:
            return [ring_copies(spot, x_view(col), tile, rs, rr, i)]

        def view(row, first, count):
            return rb.at[row, col, pl.ds(first, count), :]

        def extra_view(row, first, count):
            return eb.at[col, pl.ds(first, count), :]

        half = sent_half(spot.r, col)
        return [
            ring_copies(spot, view, rows_at(tile, half), rs, rr, i),
            ring_copies(spot, extra_view, rows_at(tile, 1 - half), es, er, i, only=col),
        ]

    def x_start(item):
        for steps in x_rings(item):
            start_pair(steps[0])

    def turned(item, offset, row):
        i, col = index_of[item], col_of(item)
        src = tb.at[row, col]
        dst = xh.at[
            pl.ds(pl.multiple_of(col * height + l * width, width), width),
            pl.ds(pl.multiple_of(row * width, width), width),
        ]
        return (
            pltpu.make_async_copy(src, dst, dl.at[1, offset, i]),
            remote(src, dst, ts.at[offset, i], tr.at[offset, i], spot.sibling),
        )

    def placed(item, offset, row):
        i, col = index_of[item], col_of(item)
        half = sent_half(row, col)

        def target(h):
            return x_view(col)(row, h * width, width)

        return (
            pltpu.make_async_copy(rb.at[row, col], target(half), dl.at[0, offset, i]),
            pltpu.make_async_copy(eb.at[col], target(1 - half), dl.at[2, 0, i]),
        )

    def turn(item, offset, row, src):
        col = col_of(item)

        @pl.when(jnp.logical_and(row != col, col != spot.r))
        def _():
            @pl.loop(0, width // BS)
            def _(strip):
                at = pl.ds(pl.multiple_of(strip * BS, BS), BS)
                tb[row, col, at, :] = src[:, at].T

            here, there_ = turned(item, offset, row)
            pl.when(row > col)(here.start)
            pl.when(row < col)(there_.start)

    def turn_done(item, offset, row):
        col = col_of(item)

        @pl.when(jnp.logical_and(row != col, col != spot.r))
        def _():
            here, there_ = turned(item, offset, row)
            pl.when(row > col)(here.wait)
            pl.when(row < col)(there_.wait)

    def turn_own(item):
        if symmetric:
            half = sent_half(spot.r, col_of(item))
            turn(item, 0, spot.r, rows_at(tile_of(0, item), half))

    def take(item):
        for steps in x_rings(item):
            pair_arrives(steps[-1])
        if symmetric:

            @pl.loop(1, rows)
            def _(offset):
                row = spot.at(offset)
                tile, extra = placed(item, offset, row)
                tile.start()
                pl.when(row == col_of(item))(extra.start)
                turn(item, offset, row, rb.at[row, col_of(item)])

    def take_done(item):
        if symmetric:
            turn_done(item, 0, spot.r)

            @pl.loop(1, rows)
            def _(offset):
                row = spot.at(offset)
                tile, extra = placed(item, offset, row)
                tile.wait()
                pl.when(row == col_of(item))(extra.wait)
                turn_done(item, offset, row)

    g_item = len(items)

    def g_ring():
        return ring_copies(spot, g_view, g_ref, rs, rr, g_item)

    def g_col_copy():
        return pltpu.make_async_copy(g_ref, g_view(spot.r, 0, height), ls.at[0, 0, len(items)])

    def spread(kind, item):
        sibling_copy(kind, item).start()
        for copy in local_copies(kind, item):
            copy.start()

    for way in (0, 1):
        when(line_sends(way, 0), lambda way=way: line_copy(0, way, 0).start())
    x_start((0, 0))
    start_pair(g_ring()[0])
    g_col_copy().start()
    for kind in (0, 1):
        spread(kind, (0, 0))
    def arrive_x(item):
        way, d = item
        line_copy(0, way, d - 1).wait_recv()
        when(line_sends(way, d) if d < cols - 1 else jnp.bool_(False), lambda: line_copy(0, way, d).start())
        x_start(item)
        spread(0, item)

    def arrive_g(item):
        way, d = item
        line_copy(1, way, d - 1).wait_recv()
        when(line_sends(way, d) if d < cols - 1 else jnp.bool_(False), lambda: line_copy(1, way, d).start())
        spread(1, item)

    def ring_on(item):
        for steps in x_rings(item):
            pass_on(steps)

    turn_own((0, 0))
    previous = [(0, 0)]
    def each(some, body):
        for item in some:
            when(there(item), lambda item=item: body(item))

    for d in range(1, cols):
        current = [(0, d), (1, d)]
        each(current, arrive_x)
        if d == 1:
            for way in (0, 1):
                when(line_sends(way, 0), line_copy(1, way, 0).start)
        else:
            each([(0, d - 1), (1, d - 1)], arrive_g)
        each(previous, ring_on)
        if d == 1:
            pass_on(g_ring())
        each(current, turn_own)
        each(previous, take)
        previous = current
    each(previous, ring_on)
    each(previous, take)
    each(previous, arrive_g)

    def finish(item):
        way, d = item
        for steps in x_rings(item):
            for pair in steps:
                pair_left(pair)
        take_done(item)
        for kind in (0, 1):
            copy = sibling_copy(kind, item)
            copy.wait_send()
            copy.wait_recv()
            for copy in local_copies(kind, item):
                copy.wait()

    each(items, finish)
    steps = g_ring()
    for pair in steps:
        pair_left(pair)
    pair_arrives(steps[-1])
    g_col_copy().wait()
    for kind in (0, 1):
        for way in (0, 1):
            for d in range(cols - 1):
                when(line_sends(way, d), lambda kind=kind, way=way, d=d: line_copy(kind, way, d).wait_send())


def share_kernel(
    rows, cols, width, p_ref, mask_ref, xr, xh, sf, pf, pc, left, right, square, rs, rr, ss, sr, ls, fs
):
    spot = Spot(rows, cols)
    height = p_ref.shape[0]
    spot.greet((spot.right, spot.left, spot.sibling))

    def fetch(col):
        slot = lax.rem(col, 2)
        src = xh.at[:, pl.ds(pl.multiple_of(col * width, width), width)]
        return pltpu.make_async_copy(src, right.at[slot], fs.at[slot])

    whole_left = pltpu.make_async_copy(xr, left, fs.at[2])
    whole_left.start()
    fetch(jnp.int32(0)).start()
    mine = p_ref.at[:, pl.ds(pl.multiple_of(spot.c * width, width), width)]

    def view(row, first, count):
        return pc.at[pl.ds(pl.multiple_of(row * height + first, 16), count), :]

    steps = ring_copies(spot, view, mine, rs, rr, 0)
    start_pair(steps[0])
    own_cols = pltpu.make_async_copy(mine, view(spot.r, 0, height), ls.at[2, 0])
    own_cols.start()

    def spread(kind, col):
        at = pl.ds(pl.multiple_of(col * width, width), width)
        src = p_ref.at[:, at] if kind == 0 else square.at[col]
        dst = (pf, sf)[kind].at[:, pl.ds(pl.multiple_of((col * 2 + spot.l) * width, width), width)]
        return (
            remote(src, dst, ss.at[kind, col], sr.at[kind, col], spot.sibling),
            pltpu.make_async_copy(src, dst, ls.at[kind, col]),
        )

    @pl.loop(0, cols)
    def _(col):
        for copy in spread(0, col):
            copy.start()

    whole_left.wait()
    block = min(2 * BS, height)

    @pl.loop(0, cols)
    def _(col):
        fetch(col).wait()
        pl.when(col + 1 < cols)(lambda: fetch(col + 1).start())
        slot = lax.rem(col, 2)
        at = pl.ds(pl.multiple_of(col * width, width), width)

        @pl.loop(0, height // block)
        def _(part):
            these = pl.ds(pl.multiple_of(part * block, block), block)
            product = jnp.dot(left[these, :], right[slot], preferred_element_type=jnp.float32)
            kept = jnp.where(mask_ref[these, at] > 0, product, 0.0)
            square[col, these, :] = kept.astype(square.dtype)

        for copy in spread(1, col):
            copy.start()

    pass_on(steps)
    pair_arrives(steps[-1])
    for pair in steps:
        pair_left(pair)
    own_cols.wait()

    @pl.loop(0, cols)
    def _(col):
        for kind in (0, 1):
            for copy in spread(kind, col):
                copy.wait()


def gather_all(rows, cols, x, g):
    height, width = x.shape
    shape = lambda a, b: jax.ShapeDtypeStruct((a, b), x.dtype)
    items = 2 * cols - 1
    dma = pltpu.SemaphoreType.DMA
    symmetric = []
    if height == 2 * width and rows == cols:
        symmetric = [
            pltpu.VMEM((rows, cols, width, width), x.dtype),
            pltpu.VMEM((cols, width, width), x.dtype),
            pltpu.VMEM((rows, cols, width, width), x.dtype),
            dma((items, rows // 2, 2)),
            dma((items, rows // 2, 2)),
            dma((rows, items)),
            dma((rows, items)),
            dma((3, rows, items)),
        ]
    return pl.pallas_call(
        lambda *refs: gather_kernel(rows, cols, *refs),
        out_shape=(
            shape(height, 2 * cols * width),
            shape(rows * height, cols * width),
            shape(height, 2 * cols * width),
            shape(height, cols * width),
            shape(rows * height, width),
        ),
        in_specs=[VMEM] * 2,
        out_specs=(ANY,) * 5,
        scratch_shapes=[
            pltpu.VMEM((cols, height, width), x.dtype),
            pltpu.VMEM((cols, height, width), x.dtype),
            dma((2, 2, cols)),
            dma((2, 2, cols)),
            dma((items + 1, rows // 2, 2)),
            dma((items + 1, rows // 2, 2)),
            dma((2, items)),
            dma((2, items)),
            dma((2, 2, items + 1)),
            *symmetric,
        ],
        compiler_params=pltpu.CompilerParams(collective_id=0, has_side_effects=True, vmem_limit_bytes=VMEM_LIMIT),
        name="gather_all",
    )(x, g)


def share(rows, cols, width, p, mask, x_rows, x_half):
    height = p.shape[0]
    depth = x_half.shape[0]
    shape = lambda a, b: jax.ShapeDtypeStruct((a, b), p.dtype)
    dma = pltpu.SemaphoreType.DMA
    return pl.pallas_call(
        lambda *refs: share_kernel(rows, cols, width, *refs),
        out_shape=(
            shape(height, 2 * cols * width),
            shape(height, 2 * cols * width),
            shape(rows * height, width),
        ),
        in_specs=[VMEM, VMEM, ANY, ANY],
        out_specs=(ANY,) * 3,
        scratch_shapes=[
            pltpu.VMEM((height, depth), p.dtype),
            pltpu.VMEM((2, depth, width), p.dtype),
            pltpu.VMEM((cols, height, width), p.dtype),
            dma((1, rows // 2, 2)),
            dma((1, rows // 2, 2)),
            dma((2, cols)),
            dma((2, cols)),
            dma((3, cols)),
            dma((3,)),
        ],
        compiler_params=pltpu.CompilerParams(
            collective_id=1, has_side_effects=True, vmem_limit_bytes=VMEM_LIMIT
        ),
        name="share",
    )(p, mask, x_rows, x_half)


def dot(a, b):
    return jnp.dot(a, b, preferred_element_type=jnp.float32)


def hits(blocks, positions):
    return (blocks[:, None] == positions[None, :] // BS).astype(jnp.bfloat16)


def mask_of(block_pattern, row_positions, col_positions):
    counted = jnp.einsum(
        "nr,nc->rc",
        hits(block_pattern[0], row_positions),
        hits(block_pattern[1], col_positions),
        preferred_element_type=jnp.float32,
    )
    return counted > 0.5


def solution(mesh):
    rows, cols, layers = mesh.shape["row"], mesh.shape["col"], mesh.shape["layer"]

    def per_device(density, cotangent, block_pattern):
        height, width = density.shape
        r, c, l = (lax.axis_index(name) for name in ("row", "col", "layer"))
        row_at = r * height + jnp.arange(height, dtype=jnp.int32)
        col_at = (c * layers + l) * width + jnp.arange(width, dtype=jnp.int32)
        along = jnp.arange(cols * width, dtype=jnp.int32)
        half_at = ((along // width) * layers + l) * width + along % width
        mask = mask_of(block_pattern, row_at, col_at)
        half_mask = mask_of(block_pattern, row_at, half_at)
        xm = jnp.where(mask, density, jnp.zeros_like(density))
        masked_grad = jnp.where(mask, cotangent, jnp.zeros_like(cotangent))
        x_rows, x_half, g_rows, g_half, g_cols = gather_all(rows, cols, xm, masked_grad)
        pulled = jnp.where(
            half_mask, 3.0 * g_half.astype(jnp.float32) - 2.0 * dot(g_rows, x_half), 0.0
        ).astype(jnp.bfloat16)
        s_rows, p_rows, p_cols = share(
            rows, cols, width, pulled, half_mask.astype(jnp.bfloat16), x_rows, x_half
        )
        x_cols = lax.dynamic_slice_in_dim(x_half, c * width, width, axis=1)
        total = -2.0 * dot(s_rows, g_cols) + dot(p_rows, x_cols) + dot(x_rows, p_cols)
        return jnp.where(mask, total, 0.0)

    return jax.shard_map(
        per_device,
        mesh=mesh,
        in_specs=(P("row", ("col", "layer")), P("row", ("col", "layer")), P()),
        out_specs=P("row", ("col", "layer")),
        check_vma=False,
    )
```

```python
import jax
import jax.numpy as jnp
from jax import lax
from jax.experimental import pallas as pl
from jax.experimental.pallas import tpu as pltpu
from jax.sharding import PartitionSpec as P

BS = 128
MESH = pl.DeviceIdType.MESH
ANY = pl.BlockSpec(memory_space=pl.ANY)
VMEM = pl.BlockSpec(memory_space=pltpu.VMEM)
VMEM_LIMIT = 48 * 2**20


def ring_place(index, size):
    upper = index // (size // 2)
    return index + upper * (size + size // 2 - 1 - 2 * index)


class Spot:
    def __init__(self, rows, cols):
        self.rows, self.cols = rows, cols
        self.r = lax.axis_index("row")
        self.c = lax.axis_index("col")
        self.l = lax.axis_index("layer")
        self.p = ring_place(self.r, rows)
        self.right = (self.at(1), self.c, self.l)
        self.left = (self.at(-1), self.c, self.l)
        self.sibling = (self.r, self.c, 1 - self.l)
        self.up = (self.r, lax.rem(self.c + 1, cols), self.l)
        self.down = (self.r, lax.rem(self.c + cols - 1, cols), self.l)

    def at(self, step):
        return ring_place(lax.rem(self.p + step + self.rows, self.rows), self.rows)

    def greet(self, others):
        barrier = pltpu.get_barrier_semaphore()
        for other in others:
            pl.semaphore_signal(barrier, inc=1, device_id=other, device_id_type=MESH)
        pl.semaphore_wait(barrier, len(others))


def remote(src, dst, send, recv, device):
    return pltpu.make_async_remote_copy(
        src_ref=src, dst_ref=dst, send_sem=send, recv_sem=recv, device_id=device, device_id_type=MESH
    )


def ring_copies(spot, view, own, sends, recvs, item, only=None):
    half_way = spot.rows // 2
    tile = own.shape[0]
    steps = []
    for step in range(1, half_way + 1):
        pair = []
        for way, (target, sign) in enumerate(((spot.right, 1), (spot.left, -1))):
            origin = spot.at(-sign * (step - 1))
            if step < half_way:
                first, count = 0, tile
            else:
                first, count = way * (tile // 2), tile // 2
            src = own.at[pl.ds(first, count), :] if step == 1 else view(origin, first, count)
            copy = remote(
                src,
                view(origin, first, count),
                sends.at[item, step - 1, way],
                recvs.at[item, step - 1, way],
                target,
            )
            if only is None:
                pair.append((copy, None, None))
            else:
                pair.append((copy, origin == only, spot.at(-sign * step) == only))
        steps.append(pair)
    return steps


def when(cond, body):
    if cond is None:
        body()
    else:
        pl.when(cond)(body)


def start_pair(pair):
    for copy, sent, _ in pair:
        when(sent, copy.start)


def pair_arrives(pair):
    for copy, _, arrives in pair:
        when(arrives, copy.wait_recv)


def pair_left(pair):
    for copy, sent, _ in pair:
        when(sent, copy.wait_send)


def pass_on(steps):
    for step in range(1, len(steps)):
        pair_arrives(steps[step - 1])
        start_pair(steps[step])


def gather_kernel(
    rows, cols, x_ref, g_ref, xr, xh, gr, gh, gc, xs, gs, zs, zr, rs, rr, ss, sr, ls, *symmetric
):
    spot = Spot(rows, cols)
    height, width = x_ref.shape
    c, l = spot.c, spot.l

    def wide(ref, col):
        return ref.at[:, pl.ds(pl.multiple_of((col * 2 + l) * width, width), width)]

    def x_view(col):
        def view(row, first, count):
            return xh.at[
                pl.ds(pl.multiple_of(row * height + first, 16), count),
                pl.ds(pl.multiple_of(col * width, width), width),
            ]

        return view

    def g_view(row, first, count):
        return gc.at[pl.ds(pl.multiple_of(row * height + first, 16), count), :]

    def slot(kind, col):
        return (xs, gs)[kind].at[col]

    def tile_of(kind, item):
        if item[1] == 0:
            return (x_ref, g_ref)[kind]
        return slot(kind, col_of(item))

    spot.greet((spot.right, spot.left, spot.sibling, spot.up, spot.down))

    items = [(0, 0)] + [(way, d) for d in range(1, cols) for way in (0, 1)]
    index_of = {item: i for i, item in enumerate(items)}

    def col_of(item):
        way, d = item
        return c - d if way == 0 else c + d

    def there(item):
        way, d = item
        if d == 0:
            return None
        return c >= d if way == 0 else c < cols - d

    def both(a, b):
        return b if a is None else jnp.logical_and(a, b)

    def line_copy(kind, way, d):
        col = c - d if way == 0 else c + d
        src = tile_of(kind, (way, d))
        target = spot.up if way == 0 else spot.down
        return remote(src, slot(kind, col), zs.at[kind, way, d], zr.at[kind, way, d], target)

    def line_sends(way, d):
        further = c < cols - 1 if way == 0 else c > 0
        return both(there((way, d)), further)

    def sibling_copy(kind, item):
        i = index_of[item]
        dst = wide((xr, gr)[kind], col_of(item))
        return remote(tile_of(kind, item), dst, ss.at[kind, i], sr.at[kind, i], spot.sibling)

    def local_copies(kind, item):
        i = index_of[item]
        col = col_of(item)
        src = tile_of(kind, item)
        if kind == 0:
            targets = (wide(xr, col), x_view(col)(spot.r, 0, height))
        else:
            targets = (wide(gr, col), gh.at[:, pl.ds(pl.multiple_of(col * width, width), width)])
        return [pltpu.make_async_copy(src, dst, ls.at[kind, j, i]) for j, dst in enumerate(targets)]

    if symmetric:
        rb, eb, tb, es, er, ts, tr, dl = symmetric

    def sent_half(row, col):
        return l + (row < col).astype(jnp.int32) * (1 - 2 * l)

    def rows_at(tile, half):
        return tile.at[pl.ds(pl.multiple_of(half * width, width), width), :]

    def x_rings(item):
        i, col, tile = index_of[item], col_of(item), tile_of(0, item)
        if not symmetric:
            return [ring_copies(spot, x_view(col), tile, rs, rr, i)]

        def view(row, first, count):
            return rb.at[row, col, pl.ds(first, count), :]

        def extra_view(row, first, count):
            return eb.at[col, pl.ds(first, count), :]

        half = sent_half(spot.r, col)
        return [
            ring_copies(spot, view, rows_at(tile, half), rs, rr, i),
            ring_copies(spot, extra_view, rows_at(tile, 1 - half), es, er, i, only=col),
        ]

    def x_start(item):
        for steps in x_rings(item):
            start_pair(steps[0])

    def turned(item, offset, row):
        i, col = index_of[item], col_of(item)
        src = tb.at[row, col]
        dst = xh.at[
            pl.ds(pl.multiple_of(col * height + l * width, width), width),
            pl.ds(pl.multiple_of(row * width, width), width),
        ]
        return (
            pltpu.make_async_copy(src, dst, dl.at[1, offset, i]),
            remote(src, dst, ts.at[offset, i], tr.at[offset, i], spot.sibling),
        )

    def placed(item, offset, row):
        i, col = index_of[item], col_of(item)
        half = sent_half(row, col)

        def target(h):
            return x_view(col)(row, h * width, width)

        return (
            pltpu.make_async_copy(rb.at[row, col], target(half), dl.at[0, offset, i]),
            pltpu.make_async_copy(eb.at[col], target(1 - half), dl.at[2, 0, i]),
        )

    def turn(item, offset, row, src):
        col = col_of(item)

        @pl.when(jnp.logical_and(row != col, col != spot.r))
        def _():
            @pl.loop(0, width // BS)
            def _(strip):
                at = pl.ds(pl.multiple_of(strip * BS, BS), BS)
                tb[row, col, at, :] = src[:, at].T

            here, there_ = turned(item, offset, row)
            pl.when(row > col)(here.start)
            pl.when(row < col)(there_.start)

    def turn_done(item, offset, row):
        col = col_of(item)

        @pl.when(jnp.logical_and(row != col, col != spot.r))
        def _():
            here, there_ = turned(item, offset, row)
            pl.when(row > col)(here.wait)
            pl.when(row < col)(there_.wait)

    def turn_own(item):
        if symmetric:
            half = sent_half(spot.r, col_of(item))
            turn(item, 0, spot.r, rows_at(tile_of(0, item), half))

    def take(item):
        for steps in x_rings(item):
            pair_arrives(steps[-1])
        if symmetric:

            @pl.loop(1, rows)
            def _(offset):
                row = spot.at(offset)
                tile, extra = placed(item, offset, row)
                tile.start()
                pl.when(row == col_of(item))(extra.start)
                turn(item, offset, row, rb.at[row, col_of(item)])

    def take_done(item):
        if symmetric:
            turn_done(item, 0, spot.r)

            @pl.loop(1, rows)
            def _(offset):
                row = spot.at(offset)
                tile, extra = placed(item, offset, row)
                tile.wait()
                pl.when(row == col_of(item))(extra.wait)
                turn_done(item, offset, row)

    g_item = len(items)

    def g_ring():
        return ring_copies(spot, g_view, g_ref, rs, rr, g_item)

    def g_col_copy():
        return pltpu.make_async_copy(g_ref, g_view(spot.r, 0, height), ls.at[0, 0, len(items)])

    def spread(kind, item):
        sibling_copy(kind, item).start()
        for copy in local_copies(kind, item):
            copy.start()

    for way in (0, 1):
        when(line_sends(way, 0), lambda way=way: line_copy(0, way, 0).start())
    x_start((0, 0))
    start_pair(g_ring()[0])
    g_col_copy().start()
    for kind in (0, 1):
        spread(kind, (0, 0))
    def arrive_x(item):
        way, d = item
        line_copy(0, way, d - 1).wait_recv()
        when(line_sends(way, d) if d < cols - 1 else jnp.bool_(False), lambda: line_copy(0, way, d).start())
        x_start(item)
        spread(0, item)

    def arrive_g(item):
        way, d = item
        line_copy(1, way, d - 1).wait_recv()
        when(line_sends(way, d) if d < cols - 1 else jnp.bool_(False), lambda: line_copy(1, way, d).start())
        spread(1, item)

    def ring_on(item):
        for steps in x_rings(item):
            pass_on(steps)

    turn_own((0, 0))
    previous = [(0, 0)]
    def each(some, body):
        for item in some:
            when(there(item), lambda item=item: body(item))

    for d in range(1, cols):
        current = [(0, d), (1, d)]
        each(current, arrive_x)
        if d == 1:
            for way in (0, 1):
                when(line_sends(way, 0), line_copy(1, way, 0).start)
        else:
            each([(0, d - 1), (1, d - 1)], arrive_g)
        each(previous, ring_on)
        if d == 1:
            pass_on(g_ring())
        each(current, turn_own)
        each(previous, take)
        previous = current
    each(previous, ring_on)
    each(previous, take)
    each(previous, arrive_g)

    def finish(item):
        way, d = item
        for steps in x_rings(item):
            for pair in steps:
                pair_left(pair)
        take_done(item)
        for kind in (0, 1):
            copy = sibling_copy(kind, item)
            copy.wait_send()
            copy.wait_recv()
            for copy in local_copies(kind, item):
                copy.wait()

    each(items, finish)
    steps = g_ring()
    for pair in steps:
        pair_left(pair)
    pair_arrives(steps[-1])
    g_col_copy().wait()
    for kind in (0, 1):
        for way in (0, 1):
            for d in range(cols - 1):
                when(line_sends(way, d), lambda kind=kind, way=way, d=d: line_copy(kind, way, d).wait_send())


def share_kernel(
    rows, cols, width, p_ref, mask_ref, xr, xh, sf, pf, pc, left, right, square, rs, rr, ss, sr, ls, fs
):
    spot = Spot(rows, cols)
    height = p_ref.shape[0]
    spot.greet((spot.right, spot.left, spot.sibling))

    def fetch(col):
        slot = lax.rem(col, 2)
        src = xh.at[:, pl.ds(pl.multiple_of(col * width, width), width)]
        return pltpu.make_async_copy(src, right.at[slot], fs.at[slot])

    whole_left = pltpu.make_async_copy(xr, left, fs.at[2])
    whole_left.start()
    fetch(jnp.int32(0)).start()
    mine = p_ref.at[:, pl.ds(pl.multiple_of(spot.c * width, width), width)]

    def view(row, first, count):
        return pc.at[pl.ds(pl.multiple_of(row * height + first, 16), count), :]

    steps = ring_copies(spot, view, mine, rs, rr, 0)
    start_pair(steps[0])
    own_cols = pltpu.make_async_copy(mine, view(spot.r, 0, height), ls.at[2, 0])
    own_cols.start()

    def spread(kind, col):
        at = pl.ds(pl.multiple_of(col * width, width), width)
        src = p_ref.at[:, at] if kind == 0 else square.at[col]
        dst = (pf, sf)[kind].at[:, pl.ds(pl.multiple_of((col * 2 + spot.l) * width, width), width)]
        return (
            remote(src, dst, ss.at[kind, col], sr.at[kind, col], spot.sibling),
            pltpu.make_async_copy(src, dst, ls.at[kind, col]),
        )

    @pl.loop(0, cols)
    def _(col):
        for copy in spread(0, col):
            copy.start()

    whole_left.wait()
    block = min(2 * BS, height)

    def square_block(col):
        fetch(col).wait()
        pl.when(col + 1 < cols)(lambda: fetch(col + 1).start())
        slot = lax.rem(col, 2)
        at = pl.ds(pl.multiple_of(col * width, width), width)

        @pl.loop(0, height // block)
        def _(part):
            these = pl.ds(pl.multiple_of(part * block, block), block)
            product = jnp.dot(left[these, :], right[slot], preferred_element_type=jnp.float32)
            kept = jnp.where(mask_ref[these, at] > 0, product, 0.0)
            square[col, these, :] = kept.astype(square.dtype)

        for copy in spread(1, col):
            copy.start()

    pl.loop(0, cols - 1)(square_block)
    pass_on(steps)
    square_block(jnp.int32(cols - 1))
    pair_arrives(steps[-1])
    for pair in steps:
        pair_left(pair)
    own_cols.wait()

    @pl.loop(0, cols)
    def _(col):
        for kind in (0, 1):
            for copy in spread(kind, col):
                copy.wait()


def gather_all(rows, cols, x, g):
    height, width = x.shape
    shape = lambda a, b: jax.ShapeDtypeStruct((a, b), x.dtype)
    items = 2 * cols - 1
    dma = pltpu.SemaphoreType.DMA
    symmetric = []
    if height == 2 * width and rows == cols:
        symmetric = [
            pltpu.VMEM((rows, cols, width, width), x.dtype),
            pltpu.VMEM((cols, width, width), x.dtype),
            pltpu.VMEM((rows, cols, width, width), x.dtype),
            dma((items, rows // 2, 2)),
            dma((items, rows // 2, 2)),
            dma((rows, items)),
            dma((rows, items)),
            dma((3, rows, items)),
        ]
    return pl.pallas_call(
        lambda *refs: gather_kernel(rows, cols, *refs),
        out_shape=(
            shape(height, 2 * cols * width),
            shape(rows * height, cols * width),
            shape(height, 2 * cols * width),
            shape(height, cols * width),
            shape(rows * height, width),
        ),
        in_specs=[VMEM] * 2,
        out_specs=(ANY,) * 5,
        scratch_shapes=[
            pltpu.VMEM((cols, height, width), x.dtype),
            pltpu.VMEM((cols, height, width), x.dtype),
            dma((2, 2, cols)),
            dma((2, 2, cols)),
            dma((items + 1, rows // 2, 2)),
            dma((items + 1, rows // 2, 2)),
            dma((2, items)),
            dma((2, items)),
            dma((2, 2, items + 1)),
            *symmetric,
        ],
        compiler_params=pltpu.CompilerParams(collective_id=0, has_side_effects=True, vmem_limit_bytes=VMEM_LIMIT),
        name="gather_all",
    )(x, g)


def share(rows, cols, width, p, mask, x_rows, x_half):
    height = p.shape[0]
    depth = x_half.shape[0]
    shape = lambda a, b: jax.ShapeDtypeStruct((a, b), p.dtype)
    dma = pltpu.SemaphoreType.DMA
    return pl.pallas_call(
        lambda *refs: share_kernel(rows, cols, width, *refs),
        out_shape=(
            shape(height, 2 * cols * width),
            shape(height, 2 * cols * width),
            shape(rows * height, width),
        ),
        in_specs=[VMEM, VMEM, ANY, ANY],
        out_specs=(ANY,) * 3,
        scratch_shapes=[
            pltpu.VMEM((height, depth), p.dtype),
            pltpu.VMEM((2, depth, width), p.dtype),
            pltpu.VMEM((cols, height, width), p.dtype),
            dma((1, rows // 2, 2)),
            dma((1, rows // 2, 2)),
            dma((2, cols)),
            dma((2, cols)),
            dma((3, cols)),
            dma((3,)),
        ],
        compiler_params=pltpu.CompilerParams(
            collective_id=1, has_side_effects=True, vmem_limit_bytes=VMEM_LIMIT
        ),
        name="share",
    )(p, mask, x_rows, x_half)


def dot(a, b):
    return jnp.dot(a, b, preferred_element_type=jnp.float32)


def hits(blocks, positions):
    return (blocks[:, None] == positions[None, :] // BS).astype(jnp.bfloat16)


def mask_of(block_pattern, row_positions, col_positions):
    counted = jnp.einsum(
        "nr,nc->rc",
        hits(block_pattern[0], row_positions),
        hits(block_pattern[1], col_positions),
        preferred_element_type=jnp.float32,
    )
    return counted > 0.5


def solution(mesh):
    rows, cols, layers = mesh.shape["row"], mesh.shape["col"], mesh.shape["layer"]

    def per_device(density, cotangent, block_pattern):
        height, width = density.shape
        r, c, l = (lax.axis_index(name) for name in ("row", "col", "layer"))
        row_at = r * height + jnp.arange(height, dtype=jnp.int32)
        col_at = (c * layers + l) * width + jnp.arange(width, dtype=jnp.int32)
        along = jnp.arange(cols * width, dtype=jnp.int32)
        half_at = ((along // width) * layers + l) * width + along % width
        mask = mask_of(block_pattern, row_at, col_at)
        half_mask = mask_of(block_pattern, row_at, half_at)
        xm = jnp.where(mask, density, jnp.zeros_like(density))
        masked_grad = jnp.where(mask, cotangent, jnp.zeros_like(cotangent))
        x_rows, x_half, g_rows, g_half, g_cols = gather_all(rows, cols, xm, masked_grad)
        pulled = jnp.where(
            half_mask, 3.0 * g_half.astype(jnp.float32) - 2.0 * dot(g_rows, x_half), 0.0
        ).astype(jnp.bfloat16)
        s_rows, p_rows, p_cols = share(
            rows, cols, width, pulled, half_mask.astype(jnp.bfloat16), x_rows, x_half
        )
        x_cols = lax.dynamic_slice_in_dim(x_half, c * width, width, axis=1)
        total = -2.0 * dot(s_rows, g_cols) + dot(p_rows, x_cols) + dot(x_rows, p_cols)
        return jnp.where(mask, total, 0.0)

    return jax.shard_map(
        per_device,
        mesh=mesh,
        in_specs=(P("row", ("col", "layer")), P("row", ("col", "layer")), P()),
        out_specs=P("row", ("col", "layer")),
        check_vma=False,
    )
```
